32 devices in a mesh: groups: 2 (over y), mem: 4 (over x, core), dp: 4 (over z).
Axes of the slice: x: 2, y: 2, z: 4, core: 2. Of those that a mesh axis runs over, the one named last changes fastest.
Arguments:
- queries: bfloat16 [8, 512, 1024], P(('groups', 'dp'), 'mem'), parts along dimension 0, may hold values from -6 to 6
- local_kv: bfloat16 [8, 512, 2, 1024], P(('groups', 'dp'), 'mem'), parts along dimension 0, may hold values from -9 to 9
- memory_kv: bfloat16 [8, 8, 8, 2, 64, 128], P(('groups', 'dp'), 'mem'), parts along dimension 0, may hold values from -9 to 9
- block_home: int32 [8, 8], P(('groups', 'dp')), parts along dimension 0, may hold values from 0 to 7, as said below
- retrieved: int32 [8, 1, 8, 16], P(('groups', 'dp')), parts along dimension 0, may hold values from -1 to 7, as said below
- stretch_pos: int32 [8, 1], P(('groups', 'dp')), parts along dimension 0, may hold values from 1 to 8, as said below
- gate_bias: float32 [8], replicated, may hold values from -2 to 2
- d_out: bfloat16 [8, 512, 1024], P(('groups', 'dp'), 'mem'), parts along dimension 0, may hold values from -12.5 to 12.5
Outputs:
- attended: bfloat16 [8, 512, 1024], P(('groups', 'dp'), 'mem'), parts along dimension 0
- grad_queries: bfloat16 [8, 512, 1024], P(('groups', 'dp'), 'mem'), parts along dimension 0
- grad_kv: bfloat16 [8, 512, 2, 1024], P(('groups', 'dp'), 'mem'), parts along dimension 0
- grad_gate: float32 [16], P('groups'), parts along dimension 0
The draws below stay inside these ranges and needn't reach their ends.
There are 2 independent parts, one for each index of `groups`. The reference program is written for one: setup_inputs(seed, part) draws one part's arguments, and reference() takes and returns one part's arrays. A program takes and returns all parts, laid end to end along the dimension named above; an argument that names none is the same for every part. Nothing has to cross between parts.
Inputs may be any that keep to these rules, and one draw needn't show every extreme that they name: For each document a permutation: block r is stored in slot block_home[r] of memory_kv, which lies on index block_home[r] // 2 of mem. `retrieved`: each list names distinct blocks first and holds -1 after them. Of the named (block, head) entries of one stretch, at most 8 are stored on any one index of mem, and in each document one index of mem stores exactly 8 of every stretch's entries. Every list names a block below its stretch's stretch_pos. Block r is visible to stretch c when r < stretch_pos[c]; the last stretch of a document sees all 8 blocks.
All inputs are finite; a program needn't handle non-finite values.
Results may differ from the reference program's by a relative error of at most 0.012.
Values may be sent and summed in bfloat16 or wider, within the bound.
A program may use at most 64 MiB of HBM per device.

```python
import jax
import jax.numpy as jnp
from jax import lax

H = 8
HD = 128
TOK_DEV = 128
STRETCH = 512
BLOCK = 64
TOPK = 16
CAP = 8
MB_DEV = 2
BATCH = 4
SEQ = 512
NCHUNK = 1
NBLK = 8


def stretch_lists(key, stored, hottest):
    owners_n = NBLK // MB_DEV
    sub_keys = jax.random.split(key, 5)
    counts = jax.random.randint(sub_keys[0], (owners_n,), 1, CAP + 1)
    counts = jnp.where(jnp.arange(owners_n, dtype=jnp.int32) == hottest, CAP, counts)
    entry_head = jax.vmap(lambda sub_key: jax.random.permutation(sub_key, H))(jax.random.split(sub_keys[1], owners_n))
    is_taken = jnp.arange(H, dtype=jnp.int32)[None, :] < counts[:, None]
    per_head = jnp.sum((entry_head[:, :, None] == jnp.arange(H, dtype=jnp.int32)[None, None, :]) & is_taken[:, :, None], axis=1)
    local_picks = jax.vmap(lambda sub_key: jax.random.permutation(sub_key, MB_DEV)[:1])(jax.random.split(sub_keys[3], owners_n * H))
    local_picks = local_picks.reshape(owners_n, H, 1)
    slot_index = jnp.arange(owners_n, dtype=jnp.int32)[:, None, None] * MB_DEV + local_picks
    block_of = stored[slot_index]
    is_live = per_head[:, :, None] > 0
    candidates = jnp.transpose(block_of, (1, 0, 2)).reshape(H, owners_n)
    cand_live = jnp.transpose(is_live, (1, 0, 2)).reshape(H, owners_n)
    shuffle = jax.vmap(lambda sub_key: jax.random.permutation(sub_key, owners_n))(jax.random.split(sub_keys[4], H))
    sort_key = jnp.where(cand_live, 0, owners_n) + shuffle
    ranking = jnp.argsort(sort_key, axis=1)
    listed = jnp.take_along_axis(jnp.where(cand_live, candidates, -1), ranking, axis=1)
    padded = jnp.concatenate([listed, jnp.full((H, TOPK - owners_n), -1, jnp.int32)], axis=1)
    lowest = jnp.min(jnp.where(cand_live, candidates, NBLK), axis=1)
    return (padded.astype(jnp.int32), (jnp.max(lowest) + 1).astype(jnp.int32))


def one_document(key):
    sub_keys = jax.random.split(key, 4)
    stored = jax.random.permutation(sub_keys[0], NBLK).astype(jnp.int32)
    home_slot = jnp.argsort(stored).astype(jnp.int32)
    hottest = jax.random.randint(sub_keys[1], (), 0, NBLK // MB_DEV)
    lists, lower = jax.vmap(lambda sub_key: stretch_lists(sub_key, stored, hottest))(jax.random.split(sub_keys[2], NCHUNK))
    spread = jax.random.randint(sub_keys[3], (NCHUNK,), 0, NBLK + 1)
    positions = lower + spread % (NBLK - lower + 1)
    positions = positions.at[NCHUNK - 1].set(NBLK)
    return (home_slot, lists, positions.astype(jnp.int32))


def catalog(key):
    doc_keys = jax.random.split(jax.random.fold_in(key, 500), BATCH)
    return jax.vmap(one_document)(doc_keys)


def draw_block_home(key, part):
    shared = catalog(key)
    return shared[0]


def draw_retrieved(key, part):
    shared = catalog(key)
    return shared[1]


def draw_stretch_pos(key, part):
    shared = catalog(key)
    return shared[2]


def draw_queries(key, part):
    key = jax.random.fold_in(key, 1)
    array_shape = (BATCH, SEQ, H, HD)
    base_values = jax.random.truncated_normal(key, -4.0, 4.0, array_shape, jnp.float32)
    return base_values.reshape(BATCH, SEQ, H * HD).astype(jnp.bfloat16)


def draw_local_kv(key, part):
    key = jax.random.fold_in(key, 2)
    sub_keys = jax.random.split(key, 3)
    array_shape = (BATCH, SEQ, H, HD)
    row_scale = jnp.exp(jax.random.uniform(sub_keys[0], (BATCH, SEQ, H, 1), jnp.float32, -1.2039728, 1.0986123))
    key_part = jax.random.truncated_normal(sub_keys[1], -3.0, 3.0, array_shape, jnp.float32) * row_scale
    value_part = 2.0 * jax.random.truncated_normal(sub_keys[2], -3.0, 3.0, array_shape, jnp.float32)
    stacked = jnp.stack([key_part, value_part], axis=2)
    return stacked.reshape(BATCH, SEQ, 2, H * HD).astype(jnp.bfloat16)


def draw_memory_kv(key, part):
    key = jax.random.fold_in(key, 3)
    sub_keys = jax.random.split(key, 3)
    array_shape = (BATCH, NBLK, H, BLOCK, HD)
    row_scale = jnp.exp(jax.random.uniform(sub_keys[0], (BATCH, NBLK, H, BLOCK, 1), jnp.float32, -1.2039728, 1.0986123))
    key_part = jax.random.truncated_normal(sub_keys[1], -3.0, 3.0, array_shape, jnp.float32) * row_scale
    value_part = 2.0 * jax.random.truncated_normal(sub_keys[2], -3.0, 3.0, array_shape, jnp.float32)
    return jnp.stack([key_part, value_part], axis=3).astype(jnp.bfloat16)


def draw_d_out(key, part):
    key = jax.random.fold_in(key, 4)
    sub_keys = jax.random.split(key, 1)
    array_shape = (BATCH, SEQ, H * HD)
    along_seq = 1.0 + 2.0 * jnp.arange(SEQ, dtype=jnp.float32) / SEQ
    along_docs = 1.0 + 2.0 * jnp.arange(BATCH, dtype=jnp.float32) / BATCH
    rising = along_docs[:, None, None] * along_seq[None, :, None] / 3.0
    base_values = jax.random.truncated_normal(sub_keys[0], -4.0, 4.0, array_shape, jnp.float32)
    return (base_values * rising).astype(jnp.bfloat16)


def setup_inputs(seed: int = 0, part: int = 0) -> dict:
    splits = jax.random.split(jax.random.key(seed), 9)
    own_keys = jax.random.split(jax.random.fold_in(splits[8], part), 9)
    return {
        "queries": draw_queries(jax.random.fold_in(jax.random.fold_in(splits[8], part), 71), part),
        "local_kv": draw_local_kv(jax.random.fold_in(jax.random.fold_in(splits[8], part), 71), part),
        "memory_kv": draw_memory_kv(jax.random.fold_in(jax.random.fold_in(splits[8], part), 71), part),
        "block_home": draw_block_home(jax.random.fold_in(jax.random.fold_in(splits[8], part), 71), part),
        "retrieved": draw_retrieved(jax.random.fold_in(jax.random.fold_in(splits[8], part), 71), part),
        "stretch_pos": draw_stretch_pos(jax.random.fold_in(jax.random.fold_in(splits[8], part), 71), part),
        "gate_bias": jnp.clip(jax.random.uniform(splits[6], (H,), jnp.float32, -2.0, 2.0), -2.0, 2.0),
        "d_out": draw_d_out(jax.random.fold_in(jax.random.fold_in(splits[8], part), 71), part),
    }


neg_large = -1e+30

def masked_softmax(scores, visible):
    scores = jnp.where(visible, scores, neg_large)
    row_top = lax.optimization_barrier(jnp.max(scores, axis=-1, keepdims=True))
    lifted = jnp.exp(scores - row_top)
    row_total = lax.optimization_barrier(jnp.sum(lifted, axis=-1, keepdims=True))
    return lax.optimization_barrier((lifted / row_total).astype(jnp.bfloat16))

def stretch_pass(query_c, kv_c, dout_c, fetched, visible, gate_value):
    inv_sqrt = HD ** (-0.5)
    query_f = query_c.astype(jnp.float32)
    mem_keys = fetched[:, :, 0].reshape(H, TOPK * BLOCK, HD).astype(jnp.float32)
    mem_vals = fetched[:, :, 1].reshape(H, TOPK * BLOCK, HD).astype(jnp.float32)
    mem_mask = jnp.repeat(visible, BLOCK, axis=1)[:, None, :]
    mem_scores = jnp.einsum('qhd,hkd->hqk', query_f, mem_keys) * inv_sqrt
    mem_probs = masked_softmax(mem_scores, mem_mask)
    mem_out = jnp.einsum('hqk,hkd->qhd', mem_probs.astype(jnp.float32), mem_vals)
    near_keys = kv_c[:, 0].astype(jnp.float32)
    near_vals = kv_c[:, 1].astype(jnp.float32)
    positions = jnp.arange(STRETCH, dtype=jnp.int32)
    near_mask = (positions[None, :] <= positions[:, None])[None]
    near_scores = jnp.einsum('qhd,khd->hqk', query_f, near_keys) * inv_sqrt
    near_probs = masked_softmax(near_scores, near_mask)
    near_out = jnp.einsum('hqk,khd->qhd', near_probs.astype(jnp.float32), near_vals)
    gate_col = gate_value[None, :, None]
    attended = (gate_col * mem_out + (1.0 - gate_col) * near_out).astype(jnp.bfloat16)
    cotangent = dout_c.astype(jnp.float32)
    mem_cot = gate_col * cotangent
    near_cot = (1.0 - gate_col) * cotangent
    gate_terms = lax.optimization_barrier(jnp.sum(cotangent * (mem_out - near_out), axis=(0, 2))) * gate_value * (1.0 - gate_value)
    mem_delta = jnp.transpose(lax.optimization_barrier(jnp.sum(mem_cot * mem_out, axis=2)))[:, :, None]
    near_delta = jnp.transpose(lax.optimization_barrier(jnp.sum(near_cot * near_out, axis=2)))[:, :, None]
    mem_low = lax.optimization_barrier(mem_cot.astype(jnp.bfloat16)).astype(jnp.float32)
    near_low = lax.optimization_barrier(near_cot.astype(jnp.bfloat16)).astype(jnp.float32)
    mem_dprobs = jnp.einsum('qhd,hkd->hqk', mem_low, mem_vals)
    mem_dscores = (mem_probs.astype(jnp.float32) * (mem_dprobs - mem_delta) * inv_sqrt).astype(jnp.bfloat16)
    near_dprobs = jnp.einsum('qhd,khd->hqk', near_low, near_vals)
    near_dscores = (near_probs.astype(jnp.float32) * (near_dprobs - near_delta) * inv_sqrt).astype(jnp.bfloat16)
    mem_dsf = lax.optimization_barrier(mem_dscores).astype(jnp.float32)
    near_dsf = lax.optimization_barrier(near_dscores).astype(jnp.float32)
    query_grad = jnp.einsum('hqk,hkd->qhd', mem_dsf, mem_keys) + jnp.einsum('hqk,khd->qhd', near_dsf, near_keys)
    grad_queries = query_grad.astype(jnp.bfloat16)
    blocks_n = STRETCH // TOK_DEV
    ds_blocks = near_dsf.reshape(H, blocks_n, TOK_DEV, STRETCH)
    probs_blocks = near_probs.astype(jnp.float32).reshape(H, blocks_n, TOK_DEV, STRETCH)
    query_blocks = query_f.reshape(blocks_n, TOK_DEV, H, HD)
    cot_blocks = near_low.reshape(blocks_n, TOK_DEV, H, HD)
    key_terms = jnp.einsum('hbqk,bqhd->bkhd', ds_blocks, query_blocks)
    value_terms = jnp.einsum('hbqk,bqhd->bkhd', probs_blocks, cot_blocks)
    kv_terms = jnp.stack([key_terms, value_terms], axis=2).astype(jnp.bfloat16)
    grad_kv = lax.optimization_barrier(jnp.sum(kv_terms.astype(jnp.float32), axis=0)).astype(jnp.bfloat16)
    return (attended, grad_queries, grad_kv, gate_terms)

def reference(queries, local_kv, memory_kv, block_home, retrieved, stretch_pos, gate_bias, d_out):
    gate_value = jax.nn.sigmoid(gate_bias)
    count = BATCH * NCHUNK
    query_all = queries.reshape(count, STRETCH, H, HD)
    kv_all = local_kv.reshape(count, STRETCH, 2, H, HD)
    dout_all = d_out.reshape(count, STRETCH, H, HD)
    ids_all = retrieved.reshape(count, H, TOPK)
    pos_all = stretch_pos.reshape(count)
    doc_all = jnp.arange(count, dtype=jnp.int32) // NCHUNK
    head_ids = jnp.arange(H, dtype=jnp.int32)[:, None]

    def one_stretch(item):
        query_c, kv_c, dout_c, block_ids, stretch_limit, doc_index = item
        home_row = block_home[doc_index]
        store = memory_kv[doc_index]
        visible = (block_ids >= 0) & (block_ids < stretch_limit)
        slot_ids = home_row[jnp.clip(block_ids, 0, NBLK - 1)]
        fetched = store[slot_ids, head_ids]
        return stretch_pass(query_c, kv_c, dout_c, fetched, visible, gate_value)
    attended, grad_queries, grad_kv, gate_terms = lax.map(one_stretch, (query_all, kv_all, dout_all, ids_all, pos_all, doc_all))
    attended = attended.reshape(BATCH, SEQ, H * HD)
    grad_queries = grad_queries.reshape(BATCH, SEQ, H * HD)
    grad_kv = grad_kv.reshape(BATCH, SEQ, 2, H * HD)
    grad_gate = lax.optimization_barrier(jnp.sum(gate_terms, axis=0))
    return (attended, grad_queries, grad_kv, grad_gate)
```

```python
import functools

import jax
import jax.numpy as jnp
from jax import lax
from jax.experimental import pallas as pl
from jax.experimental.pallas import tpu as pltpu
from jax.sharding import PartitionSpec as P

H = 8
HD = 128
TOK_DEV = 128
STRETCH = 512


neg_large = -1e30


def from_partner(block, axis, stride):
    count = lax.axis_size(axis)
    route = []
    for low in range(count):
        high = low | 1 << stride
        if high != low and high < count:
            route += [(low, high), (high, low)]
    return lax.ppermute(block, axis, route)


def masked_softmax(scores, visible):
    scores = jnp.where(visible, scores, neg_large)
    row_top = jnp.max(scores, axis=-1, keepdims=True)
    lifted = jnp.exp(scores - row_top)
    row_total = jnp.sum(lifted, axis=-1, keepdims=True)
    return lax.optimization_barrier((lifted / row_total).astype(jnp.bfloat16))


def fetch_blocks(memory_kv, slot_ids, head_ids):
    everything = lax.all_gather(memory_kv, "mem", axis=1, tiled=True)[0]
    return everything[slot_ids, head_ids]


def attend(query_heads, cotangent, fetched, visible, near_keys, near_vals, near_mask, gate_value):
    inv_sqrt = HD ** (-0.5)
    heads_here = fetched.shape[0]
    keys_n = fetched.shape[1] * fetched.shape[3]
    mem_keys = fetched[:, :, 0].reshape(heads_here, keys_n, HD)
    mem_vals = fetched[:, :, 1].reshape(heads_here, keys_n, HD)
    mem_mask = jnp.repeat(visible, fetched.shape[3], axis=1)[:, None, :]
    mem_scores = (
        jnp.einsum("qhd,hkd->hqk", query_heads, mem_keys, preferred_element_type=jnp.float32)
        * inv_sqrt
    )
    mem_probs = masked_softmax(mem_scores, mem_mask)
    mem_out = jnp.einsum("hqk,hkd->qhd", mem_probs, mem_vals, preferred_element_type=jnp.float32)
    near_scores = (
        jnp.einsum("qhd,khd->hqk", query_heads, near_keys, preferred_element_type=jnp.float32)
        * inv_sqrt
    )
    near_probs = masked_softmax(near_scores, near_mask)
    near_out = jnp.einsum("hqk,khd->qhd", near_probs, near_vals, preferred_element_type=jnp.float32)
    gate_col = gate_value[None, :, None]
    mixed = gate_col * mem_out + (1.0 - gate_col) * near_out
    mem_grad_out = gate_col * cotangent
    near_grad_out = (1.0 - gate_col) * cotangent
    gate_terms = (
        jnp.sum(cotangent * (mem_out - near_out), axis=(0, 2)) * gate_value * (1.0 - gate_value)
    )
    mem_delta = jnp.transpose(jnp.sum(mem_grad_out * mem_out, axis=2))[:, :, None]
    near_delta = jnp.transpose(jnp.sum(near_grad_out * near_out, axis=2))[:, :, None]
    mem_grad_low = mem_grad_out.astype(jnp.bfloat16)
    near_grad_low = near_grad_out.astype(jnp.bfloat16)
    mem_dprobs = jnp.einsum(
        "qhd,hkd->hqk", mem_grad_low, mem_vals, preferred_element_type=jnp.float32
    )
    mem_dscores = (mem_probs.astype(jnp.float32) * (mem_dprobs - mem_delta) * inv_sqrt).astype(
        jnp.bfloat16
    )
    near_dprobs = jnp.einsum(
        "qhd,khd->hqk", near_grad_low, near_vals, preferred_element_type=jnp.float32
    )
    near_dscores = (near_probs.astype(jnp.float32) * (near_dprobs - near_delta) * inv_sqrt).astype(
        jnp.bfloat16
    )
    query_grad = jnp.einsum(
        "hqk,hkd->qhd", mem_dscores, mem_keys, preferred_element_type=jnp.float32
    )
    query_grad = query_grad + jnp.einsum(
        "hqk,khd->qhd", near_dscores, near_keys, preferred_element_type=jnp.float32
    )
    return (mixed, query_grad, near_dscores, near_probs, near_grad_low, gate_terms)


def regroup(pieces):
    piece_count = pieces.shape[0]
    for bit_number in range(piece_count.bit_length() - 1):
        moving_rows = jnp.asarray(
            [k for k in range(piece_count) if k >> bit_number & 1], dtype=jnp.int32
        )
        arrived = from_partner(pieces[moving_rows], "mem", bit_number)
        pieces = pieces.at[moving_rows].set(arrived)
    return pieces


def per_device(queries, local_kv, memory_kv, block_home, retrieved, stretch_pos, gate_bias, d_out):
    my_index = lax.axis_index("mem")
    per_stretch = STRETCH // TOK_DEV
    rank_in_span = my_index % per_stretch
    stretch_index = my_index // per_stretch
    block_ids_all = lax.dynamic_index_in_dim(retrieved[0], stretch_index, 0, keepdims=False)
    stretch_limit = lax.dynamic_index_in_dim(stretch_pos[0], stretch_index, 0, keepdims=False)
    gate_value = jax.nn.sigmoid(gate_bias)
    head_group = H // per_stretch
    rank_order = rank_in_span ^ jnp.arange(per_stretch, dtype=jnp.int32)
    packed = jnp.concatenate(
        [
            queries[0].reshape(TOK_DEV, 1, H, HD),
            local_kv[0].reshape(TOK_DEV, 2, H, HD),
            d_out[0].reshape(TOK_DEV, 1, H, HD),
        ],
        axis=1,
    )
    by_rank = jnp.transpose(
        packed.reshape(TOK_DEV, 4, per_stretch, head_group, HD), (2, 0, 1, 3, 4)
    )
    gathered = regroup(by_rank[rank_order])[rank_order].reshape(STRETCH, 4, head_group, HD)
    query_heads = gathered[:, 0]
    first_head = rank_in_span * head_group
    head_ids = (first_head + jnp.arange(head_group, dtype=jnp.int32))[:, None]
    block_ids = lax.dynamic_slice_in_dim(block_ids_all, first_head, head_group, 0)
    visible = (block_ids >= 0) & (block_ids < stretch_limit)
    slot_ids = block_home[0][jnp.clip(block_ids, 0, block_home.shape[1] - 1)]
    fetched = fetch_blocks(memory_kv, slot_ids, head_ids)
    positions = jnp.arange(STRETCH, dtype=jnp.int32)
    near_mask = (positions[None, :] <= positions[:, None])[None]
    gate_mine = lax.dynamic_slice_in_dim(gate_value, first_head, head_group, 0)
    cotangent = gathered[:, 3].astype(jnp.float32)
    mixed, query_grad, near_dscores, near_probs, near_grad_low, gate_terms = attend(
        query_heads,
        cotangent,
        fetched,
        visible,
        gathered[:, 1],
        gathered[:, 2],
        near_mask,
        gate_mine,
    )
    ds_blocks = near_dscores.reshape(head_group, per_stretch, TOK_DEV, STRETCH)
    probs_blocks = near_probs.reshape(head_group, per_stretch, TOK_DEV, STRETCH)
    query_blocks = query_heads.reshape(per_stretch, TOK_DEV, head_group, HD)
    cot_blocks = near_grad_low.reshape(per_stretch, TOK_DEV, head_group, HD)
    key_terms = jnp.einsum(
        "hbqk,bqhd->bkhd", ds_blocks, query_blocks, preferred_element_type=jnp.float32
    ).astype(jnp.bfloat16)
    value_terms = jnp.einsum(
        "hbqk,bqhd->bkhd", probs_blocks, cot_blocks, preferred_element_type=jnp.float32
    ).astype(jnp.bfloat16)
    key_grad = jnp.sum(key_terms.astype(jnp.float32), axis=0).astype(jnp.bfloat16)
    value_grad = jnp.sum(value_terms.astype(jnp.float32), axis=0).astype(jnp.bfloat16)
    outgoing = jnp.stack(
        [mixed.astype(jnp.bfloat16), query_grad.astype(jnp.bfloat16), key_grad, value_grad], axis=1
    )
    outgoing = outgoing.reshape(per_stretch, TOK_DEV, 4, head_group, HD)
    returned = regroup(outgoing[rank_order])[rank_order]
    results = jnp.transpose(returned, (1, 2, 0, 3, 4)).reshape(TOK_DEV, 4, H * HD)
    attended = results[:, 0][None]
    grad_queries = results[:, 1][None]
    grad_kv = results[:, 2:4][None]
    gate_full = lax.dynamic_update_slice_in_dim(
        jnp.zeros((H,), jnp.float32), gate_terms, first_head, 0
    )
    grad_gate = lax.psum(gate_full, ("mem", "dp"))
    return (attended, grad_queries, grad_kv, grad_gate)


MESH_ID = pl.DeviceIdType.MESH
SCALE = HD ** (-0.5)
HG = H // 2


def dot_nt(a, b):
    return lax.dot_general(a, b, (((1,), (1,)), ((), ())), preferred_element_type=jnp.float32)


def dot_tn(a, b):
    return lax.dot_general(a, b, (((0,), (0,)), ((), ())), preferred_element_type=jnp.float32)


def dot_nn(a, b):
    return jnp.dot(a, b, preferred_element_type=jnp.float32)


def probs_of(scores):
    top = jnp.max(scores, axis=1, keepdims=True)
    lifted = jnp.exp(scores - top)
    return lifted * (1.0 / jnp.sum(lifted, axis=1, keepdims=True))


def layer_kernel(
    n_dp,
    q_ref,
    d_ref,
    kv_ref,
    mem_ref,
    home_ref,
    lists_ref,
    limit_ref,
    bias_ref,
    att_ref,
    dq_ref,
    gkv_ref,
    gate_ref,
    qb,
    db,
    kvb,
    memb,
    mask_s,
    att_s,
    dq_s,
    gkv_s,
    gx_s,
    gx,
    gate_s,
    gate_m,
    gate_d,
    send_sem,
    recv_sem,
    local_sem,
):
    me = lax.axis_index("mem")
    dp = lax.axis_index("dp")
    x = me // 2
    c = me % 2
    o = 1 - c
    mate = 2 * x + o
    far = 2 * (1 - x)
    bf = jnp.bfloat16

    def remote(src, dst, send_k, recv_k, device):
        return pltpu.make_async_remote_copy(
            src_ref=src,
            dst_ref=dst,
            send_sem=send_sem.at[send_k],
            recv_sem=recv_sem.at[recv_k],
            device_id=device,
            device_id_type=MESH_ID,
        )

    def lanes(first, count):
        return pl.ds(pl.multiple_of(first * HD, HD), count * HD)

    barrier = pltpu.get_barrier_semaphore()
    for k in range(1, 4):
        pl.semaphore_signal(
            barrier, inc=1, device_id={"mem": (me + k) % 4}, device_id_type=MESH_ID
        )
    for k in range(1, n_dp):
        pl.semaphore_signal(
            barrier, inc=1, device_id={"dp": (dp + k) % n_dp}, device_id_type=MESH_ID
        )

    locals_ = [
        pltpu.make_async_copy(q_ref.at[:, lanes(c * HG, HG)], qb.at[c], local_sem.at[0]),
        pltpu.make_async_copy(d_ref.at[:, lanes(c * HG, HG)], db.at[c], local_sem.at[1]),
        pltpu.make_async_copy(kv_ref.at[pl.ds(c * HG, HG)], kvb.at[me], local_sem.at[2]),
        pltpu.make_async_copy(mem_ref.at[:, pl.ds(c * HG, HG)], memb.at[me], local_sem.at[3]),
    ]
    for copy in locals_:
        copy.start()

    pl.semaphore_wait(barrier, 2 + n_dp)

    core_copies = [
        remote(q_ref.at[:, lanes(o * HG, HG)], qb.at[c], 0, 0, {"mem": mate}),
        remote(d_ref.at[:, lanes(o * HG, HG)], db.at[c], 1, 1, {"mem": mate}),
        remote(kv_ref.at[pl.ds(o * HG, HG)], kvb.at[me], 2, 2, {"mem": mate}),
        remote(mem_ref.at[:, pl.ds(o * HG, HG)], memb.at[me], 3, 3, {"mem": mate}),
    ]

    def kv_copy(to, hh):
        return remote(
            kv_ref.at[to * HG + hh],
            kvb.at[me, hh],
            4 + to * HG + hh,
            4 + c * HG + hh,
            {"mem": far + to},
        )

    def mem_copy(to, hh):
        return remote(
            mem_ref.at[:, to * HG + hh],
            memb.at[me, :, hh],
            12 + to * HG + hh,
            12 + c * HG + hh,
            {"mem": far + to},
        )

    @pl.when(x == 0)
    def _():
        for hh in range(HG):
            for to in range(2):
                kv_copy(to, hh).start()
            for to in range(2):
                mem_copy(to, hh).start()

    @pl.when(x == 1)
    def _():
        for hh in range(HG):
            for to in range(2):
                mem_copy(to, hh).start()

    for copy in core_copies:
        copy.start()

    slots = 2 * 4
    key_slot = lax.broadcasted_iota(jnp.int32, (H, slots * 64), 1) // 64
    block_of = jnp.zeros((H, slots * 64), jnp.int32)
    for r in range(slots):
        block_of = jnp.where(key_slot == home_ref[0, r], r, block_of)
    named = jnp.zeros((H, slots * 64), jnp.bool_)
    for j in range(slots):
        named = named | (block_of == lists_ref[0, 0, :, j : j + 1])
    mask_s[...] = jnp.where(named & (block_of < limit_ref[0, 0]), 0.0, neg_large)
    gate_s[...] = jnp.zeros_like(gate_s)

    def res_copy(kind, hh):
        head = c * HG + hh
        if kind == 0:
            return remote(
                att_s.at[o, hh], att_ref.at[:, lanes(head, 1)], 20 + hh, 20 + hh, {"mem": mate}
            )
        if kind == 1:
            return remote(
                dq_s.at[o, hh], dq_ref.at[:, lanes(head, 1)], 24 + hh, 24 + hh, {"mem": mate}
            )
        return remote(gkv_s.at[o, hh], gkv_ref.at[head], 28 + hh, 28 + hh, {"mem": mate})

    def gx_copy(to, hh):
        return remote(
            gx_s.at[to, hh],
            gx.at[c * HG + hh],
            32 + to * HG + hh,
            32 + c * HG + hh,
            {"mem": far + to},
        )

    def own_copy(kind, hh):
        head = c * HG + hh
        sem = local_sem.at[4 + kind * HG + hh]
        if kind == 0:
            return pltpu.make_async_copy(att_s.at[c, hh], att_ref.at[:, lanes(head, 1)], sem)
        if kind == 1:
            return pltpu.make_async_copy(dq_s.at[c, hh], dq_ref.at[:, lanes(head, 1)], sem)
        return pltpu.make_async_copy(gkv_s.at[c, hh], gkv_ref.at[head], sem)

    for copy in locals_:
        copy.wait()
    for copy in core_copies:
        copy.wait_recv()

    def one_head(hh, later):
        rows = 2 * TOK_DEV
        keys_n = 2 * TOK_DEV * (1 + later)
        first = 0 if later else 0
        head = c * HG + hh
        query = qb[:, :, hh * HD : (hh + 1) * HD].reshape(rows, HD)
        dout = db[:, :, hh * HD : (hh + 1) * HD].reshape(rows, HD).astype(jnp.float32)
        near_keys = kvb[first : first + keys_n // TOK_DEV, hh, 0].reshape(keys_n, HD)
        near_vals = kvb[first : first + keys_n // TOK_DEV, hh, 1].reshape(keys_n, HD)
        mem_keys = memb[:, :, hh, 0].reshape(slots * 64, HD)
        mem_vals = memb[:, :, hh, 1].reshape(slots * 64, HD)
        gate = 1.0 / (1.0 + jnp.exp(-jnp.full((1, HD), bias_ref[head], jnp.float32)))
        row = lax.broadcasted_iota(jnp.int32, (rows, keys_n), 0)
        col = lax.broadcasted_iota(jnp.int32, (rows, keys_n), 1)
        causal = col <= row + (keys_n - rows)
        near_probs = probs_of(
            jnp.where(causal, dot_nt(query, near_keys) * SCALE, neg_large)
        )
        near_low = near_probs.astype(bf)
        near_out = dot_nn(near_low, near_vals)
        mem_probs = probs_of(dot_nt(query, mem_keys) * SCALE + mask_s[pl.ds(head, 1), :])
        mem_out = dot_nn(mem_probs.astype(bf), mem_vals)
        mixed = (gate * mem_out + (1.0 - gate) * near_out).astype(bf)
        att_s[:, hh] = mixed.reshape(2, TOK_DEV, HD)
        gate_s[pl.ds(head, 1), :] = (
            jnp.sum(dout * (mem_out - near_out), axis=0, keepdims=True) * gate * (1.0 - gate)
        )
        mem_cot = gate * dout
        near_cot = (1.0 - gate) * dout
        mem_delta = jnp.sum(mem_cot * mem_out, axis=1, keepdims=True)
        near_delta = jnp.sum(near_cot * near_out, axis=1, keepdims=True)
        near_cot16 = near_cot.astype(bf)
        near_ds = (
            near_probs * ((dot_nt(near_cot16, near_vals) - near_delta) * SCALE)
        ).astype(bf)
        key_grad = dot_tn(near_ds, query).astype(bf)
        val_grad = dot_tn(near_low, near_cot16).astype(bf)
        split = keys_n - rows
        gkv_s[:, hh, 0] = key_grad[split:].reshape(2, TOK_DEV, HD)
        gkv_s[:, hh, 1] = val_grad[split:].reshape(2, TOK_DEV, HD)
        if later:
            gx_s[:, hh, 0] = key_grad[:split].reshape(2, TOK_DEV, HD)
            gx_s[:, hh, 1] = val_grad[:split].reshape(2, TOK_DEV, HD)
            for to in range(2):
                gx_copy(to, hh).start()
        mem_ds = (
            mem_probs * ((dot_nt(mem_cot.astype(bf), mem_vals) - mem_delta) * SCALE)
        ).astype(bf)
        query_grad = dot_nn(mem_ds, mem_keys) + dot_nn(near_ds, near_keys)
        dq_s[:, hh] = query_grad.astype(bf).reshape(2, TOK_DEV, HD)
        for kind in range(3):
            res_copy(kind, hh).start()
            own_copy(kind, hh).start()

    @pl.when(x == 0)
    def _():
        for hh in range(HG):
            for frm in range(2):
                remote(
                    mem_ref.at[:, 0], memb.at[2 + frm, :, hh], 0, 12 + frm * HG + hh, {"mem": mate}
                ).wait_recv()
            one_head(hh, False)

    @pl.when(x == 1)
    def _():
        for hh in range(HG):
            for frm in range(2):
                remote(
                    kv_ref.at[0], kvb.at[frm, hh], 0, 4 + frm * HG + hh, {"mem": mate}
                ).wait_recv()
                remote(
                    mem_ref.at[:, 0], memb.at[frm, :, hh], 0, 12 + frm * HG + hh, {"mem": mate}
                ).wait_recv()
            one_head(hh, True)

    gate_mem = [
        remote(gate_s, gate_m.at[k - 1], 40 + k, 40 + k, {"mem": (me + k) % 4})
        for k in range(1, 4)
    ]
    for copy in gate_mem:
        copy.start()
    for copy in gate_mem:
        copy.wait()
    gate_s2 = gate_d.at[0]
    gate_s2[...] = gate_s[...] + gate_m[0] + gate_m[1] + gate_m[2]
    gate_dp = [
        remote(gate_s2, gate_d.at[k], 43 + k, 43 + k, {"dp": (dp + k) % n_dp})
        for k in range(1, n_dp)
    ]
    for copy in gate_dp:
        copy.start()

    for kind in range(3):
        for hh in range(HG):
            own_copy(kind, hh).wait()
            copy = res_copy(kind, hh)
            copy.wait_send()
    for hh in range(HG):
        other = o * HG + hh
        remote(
            att_s.at[0, 0], att_ref.at[:, lanes(other, 1)], 0, 20 + hh, {"mem": mate}
        ).wait_recv()
        remote(
            dq_s.at[0, 0], dq_ref.at[:, lanes(other, 1)], 0, 24 + hh, {"mem": mate}
        ).wait_recv()
        remote(gkv_s.at[0, 0], gkv_ref.at[other], 0, 28 + hh, {"mem": mate}).wait_recv()

    @pl.when(x == 0)
    def _():
        for hh in range(HG):
            for to in range(2):
                kv_copy(to, hh).wait_send()
        for hh in range(HG):
            for frm in range(2):
                head = frm * HG + hh
                remote(
                    gkv_s.at[0, 0], gx.at[head], 0, 32 + head, {"mem": mate}
                ).wait_recv()
                gkv_ref[head] = (
                    gkv_ref[head].astype(jnp.float32) + gx[head].astype(jnp.float32)
                ).astype(bf)

    @pl.when(x == 1)
    def _():
        for hh in range(HG):
            for to in range(2):
                gx_copy(to, hh).wait_send()

    for hh in range(HG):
        for to in range(2):
            mem_copy(to, hh).wait_send()
    for copy in core_copies:
        copy.wait_send()
    for copy in gate_dp:
        copy.wait()
    total = gate_d[0]
    for k in range(1, n_dp):
        total = total + gate_d[k]
    summed = jnp.broadcast_to(jnp.sum(total, axis=1, keepdims=True), (H, HD))
    eye = lax.broadcasted_iota(jnp.int32, (H, HD), 0) == lax.broadcasted_iota(
        jnp.int32, (H, HD), 1
    )
    gate_ref[...] = jnp.sum(jnp.where(eye, summed, 0.0), axis=0, keepdims=True)


def one_stretch_per_document(
    n_dp, queries, local_kv, memory_kv, block_home, retrieved, stretch_pos, gate_bias, d_out
):
    bf = jnp.bfloat16
    kv_heads = jnp.transpose(local_kv.reshape(TOK_DEV, 2, H, HD), (2, 1, 0, 3))
    vmem = pl.BlockSpec(memory_space=pltpu.VMEM)
    smem = pl.BlockSpec(memory_space=pltpu.SMEM)
    n_sems = 44 + n_dp
    attended, grad_queries, grad_kv, grad_gate = pl.pallas_call(
        functools.partial(layer_kernel, n_dp),
        out_shape=(
            jax.ShapeDtypeStruct((TOK_DEV, H * HD), bf),
            jax.ShapeDtypeStruct((TOK_DEV, H * HD), bf),
            jax.ShapeDtypeStruct((H, 2, TOK_DEV, HD), bf),
            jax.ShapeDtypeStruct((1, HD), jnp.float32),
        ),
        in_specs=[vmem, vmem, vmem, vmem, smem, vmem, smem, smem],
        out_specs=(vmem, vmem, vmem, vmem),
        scratch_shapes=[
            pltpu.VMEM((2, TOK_DEV, HG * HD), bf),
            pltpu.VMEM((2, TOK_DEV, HG * HD), bf),
            pltpu.VMEM((4, HG, 2, TOK_DEV, HD), bf),
            pltpu.VMEM((4, 2, HG, 2, 64, HD), bf),
            pltpu.VMEM((H, 512), jnp.float32),
            pltpu.VMEM((2, HG, TOK_DEV, HD), bf),
            pltpu.VMEM((2, HG, TOK_DEV, HD), bf),
            pltpu.VMEM((2, HG, 2, TOK_DEV, HD), bf),
            pltpu.VMEM((2, HG, 2, TOK_DEV, HD), bf),
            pltpu.VMEM((H, 2, TOK_DEV, HD), bf),
            pltpu.VMEM((H, HD), jnp.float32),
            pltpu.VMEM((3, H, HD), jnp.float32),
            pltpu.VMEM((n_dp, H, HD), jnp.float32),
            pltpu.SemaphoreType.DMA((n_sems,)),
            pltpu.SemaphoreType.DMA((n_sems,)),
            pltpu.SemaphoreType.DMA((4 + 3 * HG,)),
        ],
        compiler_params=pltpu.CompilerParams(
            collective_id=0, has_side_effects=True, vmem_limit_bytes=40 * 1024 * 1024
        ),
    )(
        queries[0],
        d_out[0],
        kv_heads,
        memory_kv[0],
        block_home,
        retrieved,
        stretch_pos,
        gate_bias,
    )
    grad_kv = jnp.transpose(grad_kv, (2, 1, 0, 3)).reshape(1, TOK_DEV, 2, H * HD)
    return (attended[None], grad_queries[None], grad_kv, grad_gate[0, :H])


def solution(mesh):
    body = per_device
    if mesh.shape["mem"] == STRETCH // TOK_DEV:
        body = functools.partial(one_stretch_per_document, mesh.shape["dp"])
    in_specs = (
        P(("groups", "dp"), "mem", None),
        P(("groups", "dp"), "mem", None, None),
        P(("groups", "dp"), "mem", None, None, None, None),
        P(("groups", "dp"), None),
        P(("groups", "dp"), None, None, None),
        P(("groups", "dp"), None),
        P(),
        P(("groups", "dp"), "mem", None),
    )
    out_specs = (
        P(("groups", "dp"), "mem", None),
        P(("groups", "dp"), "mem", None),
        P(("groups", "dp"), "mem", None, None),
        P("groups"),
    )
    return jax.shard_map(
        body, mesh=mesh, in_specs=in_specs, out_specs=out_specs, check_vma=False
    )
```

```python
import functools

import jax
import jax.numpy as jnp
from jax import lax
from jax.experimental import pallas as pl
from jax.experimental.pallas import tpu as pltpu
from jax.sharding import PartitionSpec as P

H = 8
HD = 128
TOK_DEV = 128
STRETCH = 512


neg_large = -1e30


def from_partner(block, axis, stride):
    count = lax.axis_size(axis)
    route = []
    for low in range(count):
        high = low | 1 << stride
        if high != low and high < count:
            route += [(low, high), (high, low)]
    return lax.ppermute(block, axis, route)


def masked_softmax(scores, visible):
    scores = jnp.where(visible, scores, neg_large)
    row_top = jnp.max(scores, axis=-1, keepdims=True)
    lifted = jnp.exp(scores - row_top)
    row_total = jnp.sum(lifted, axis=-1, keepdims=True)
    return lax.optimization_barrier((lifted / row_total).astype(jnp.bfloat16))


def fetch_blocks(memory_kv, slot_ids, head_ids):
    everything = lax.all_gather(memory_kv, "mem", axis=1, tiled=True)[0]
    return everything[slot_ids, head_ids]


def attend(query_heads, cotangent, fetched, visible, near_keys, near_vals, near_mask, gate_value):
    inv_sqrt = HD ** (-0.5)
    heads_here = fetched.shape[0]
    keys_n = fetched.shape[1] * fetched.shape[3]
    mem_keys = fetched[:, :, 0].reshape(heads_here, keys_n, HD)
    mem_vals = fetched[:, :, 1].reshape(heads_here, keys_n, HD)
    mem_mask = jnp.repeat(visible, fetched.shape[3], axis=1)[:, None, :]
    mem_scores = (
        jnp.einsum("qhd,hkd->hqk", query_heads, mem_keys, preferred_element_type=jnp.float32)
        * inv_sqrt
    )
    mem_probs = masked_softmax(mem_scores, mem_mask)
    mem_out = jnp.einsum("hqk,hkd->qhd", mem_probs, mem_vals, preferred_element_type=jnp.float32)
    near_scores = (
        jnp.einsum("qhd,khd->hqk", query_heads, near_keys, preferred_element_type=jnp.float32)
        * inv_sqrt
    )
    near_probs = masked_softmax(near_scores, near_mask)
    near_out = jnp.einsum("hqk,khd->qhd", near_probs, near_vals, preferred_element_type=jnp.float32)
    gate_col = gate_value[None, :, None]
    mixed = gate_col * mem_out + (1.0 - gate_col) * near_out
    mem_grad_out = gate_col * cotangent
    near_grad_out = (1.0 - gate_col) * cotangent
    gate_terms = (
        jnp.sum(cotangent * (mem_out - near_out), axis=(0, 2)) * gate_value * (1.0 - gate_value)
    )
    mem_delta = jnp.transpose(jnp.sum(mem_grad_out * mem_out, axis=2))[:, :, None]
    near_delta = jnp.transpose(jnp.sum(near_grad_out * near_out, axis=2))[:, :, None]
    mem_grad_low = mem_grad_out.astype(jnp.bfloat16)
    near_grad_low = near_grad_out.astype(jnp.bfloat16)
    mem_dprobs = jnp.einsum(
        "qhd,hkd->hqk", mem_grad_low, mem_vals, preferred_element_type=jnp.float32
    )
    mem_dscores = (mem_probs.astype(jnp.float32) * (mem_dprobs - mem_delta) * inv_sqrt).astype(
        jnp.bfloat16
    )
    near_dprobs = jnp.einsum(
        "qhd,khd->hqk", near_grad_low, near_vals, preferred_element_type=jnp.float32
    )
    near_dscores = (near_probs.astype(jnp.float32) * (near_dprobs - near_delta) * inv_sqrt).astype(
        jnp.bfloat16
    )
    query_grad = jnp.einsum(
        "hqk,hkd->qhd", mem_dscores, mem_keys, preferred_element_type=jnp.float32
    )
    query_grad = query_grad + jnp.einsum(
        "hqk,khd->qhd", near_dscores, near_keys, preferred_element_type=jnp.float32
    )
    return (mixed, query_grad, near_dscores, near_probs, near_grad_low, gate_terms)


def regroup(pieces):
    piece_count = pieces.shape[0]
    for bit_number in range(piece_count.bit_length() - 1):
        moving_rows = jnp.asarray(
            [k for k in range(piece_count) if k >> bit_number & 1], dtype=jnp.int32
        )
        arrived = from_partner(pieces[moving_rows], "mem", bit_number)
        pieces = pieces.at[moving_rows].set(arrived)
    return pieces


def per_device(queries, local_kv, memory_kv, block_home, retrieved, stretch_pos, gate_bias, d_out):
    my_index = lax.axis_index("mem")
    per_stretch = STRETCH // TOK_DEV
    rank_in_span = my_index % per_stretch
    stretch_index = my_index // per_stretch
    block_ids_all = lax.dynamic_index_in_dim(retrieved[0], stretch_index, 0, keepdims=False)
    stretch_limit = lax.dynamic_index_in_dim(stretch_pos[0], stretch_index, 0, keepdims=False)
    gate_value = jax.nn.sigmoid(gate_bias)
    head_group = H // per_stretch
    rank_order = rank_in_span ^ jnp.arange(per_stretch, dtype=jnp.int32)
    packed = jnp.concatenate(
        [
            queries[0].reshape(TOK_DEV, 1, H, HD),
            local_kv[0].reshape(TOK_DEV, 2, H, HD),
            d_out[0].reshape(TOK_DEV, 1, H, HD),
        ],
        axis=1,
    )
    by_rank = jnp.transpose(
        packed.reshape(TOK_DEV, 4, per_stretch, head_group, HD), (2, 0, 1, 3, 4)
    )
    gathered = regroup(by_rank[rank_order])[rank_order].reshape(STRETCH, 4, head_group, HD)
    query_heads = gathered[:, 0]
    first_head = rank_in_span * head_group
    head_ids = (first_head + jnp.arange(head_group, dtype=jnp.int32))[:, None]
    block_ids = lax.dynamic_slice_in_dim(block_ids_all, first_head, head_group, 0)
    visible = (block_ids >= 0) & (block_ids < stretch_limit)
    slot_ids = block_home[0][jnp.clip(block_ids, 0, block_home.shape[1] - 1)]
    fetched = fetch_blocks(memory_kv, slot_ids, head_ids)
    positions = jnp.arange(STRETCH, dtype=jnp.int32)
    near_mask = (positions[None, :] <= positions[:, None])[None]
    gate_mine = lax.dynamic_slice_in_dim(gate_value, first_head, head_group, 0)
    cotangent = gathered[:, 3].astype(jnp.float32)
    mixed, query_grad, near_dscores, near_probs, near_grad_low, gate_terms = attend(
        query_heads,
        cotangent,
        fetched,
        visible,
        gathered[:, 1],
        gathered[:, 2],
        near_mask,
        gate_mine,
    )
    ds_blocks = near_dscores.reshape(head_group, per_stretch, TOK_DEV, STRETCH)
    probs_blocks = near_probs.reshape(head_group, per_stretch, TOK_DEV, STRETCH)
    query_blocks = query_heads.reshape(per_stretch, TOK_DEV, head_group, HD)
    cot_blocks = near_grad_low.reshape(per_stretch, TOK_DEV, head_group, HD)
    key_terms = jnp.einsum(
        "hbqk,bqhd->bkhd", ds_blocks, query_blocks, preferred_element_type=jnp.float32
    ).astype(jnp.bfloat16)
    value_terms = jnp.einsum(
        "hbqk,bqhd->bkhd", probs_blocks, cot_blocks, preferred_element_type=jnp.float32
    ).astype(jnp.bfloat16)
    key_grad = jnp.sum(key_terms.astype(jnp.float32), axis=0).astype(jnp.bfloat16)
    value_grad = jnp.sum(value_terms.astype(jnp.float32), axis=0).astype(jnp.bfloat16)
    outgoing = jnp.stack(
        [mixed.astype(jnp.bfloat16), query_grad.astype(jnp.bfloat16), key_grad, value_grad], axis=1
    )
    outgoing = outgoing.reshape(per_stretch, TOK_DEV, 4, head_group, HD)
    returned = regroup(outgoing[rank_order])[rank_order]
    results = jnp.transpose(returned, (1, 2, 0, 3, 4)).reshape(TOK_DEV, 4, H * HD)
    attended = results[:, 0][None]
    grad_queries = results[:, 1][None]
    grad_kv = results[:, 2:4][None]
    gate_full = lax.dynamic_update_slice_in_dim(
        jnp.zeros((H,), jnp.float32), gate_terms, first_head, 0
    )
    grad_gate = lax.psum(gate_full, ("mem", "dp"))
    return (attended, grad_queries, grad_kv, grad_gate)


MESH_ID = pl.DeviceIdType.MESH
SCALE = HD ** (-0.5)
CAP = 8
HG = H // 2


def dot_nt(a, b):
    return lax.dot_general(a, b, (((1,), (1,)), ((), ())), preferred_element_type=jnp.float32)


def dot_tn(a, b):
    return lax.dot_general(a, b, (((0,), (0,)), ((), ())), preferred_element_type=jnp.float32)


def dot_nn(a, b):
    return jnp.dot(a, b, preferred_element_type=jnp.float32)


def probs_of(scores):
    top = jnp.max(scores, axis=1, keepdims=True)
    lifted = jnp.exp(scores - top)
    return lifted * (1.0 / jnp.sum(lifted, axis=1, keepdims=True))


def layer_kernel(
    n_dp,
    q_ref,
    d_ref,
    kv_ref,
    mem_ref,
    home_ref,
    lists_ref,
    ids_ref,
    limit_ref,
    bias_ref,
    att_ref,
    dq_ref,
    gkv_ref,
    gate_ref,
    qb,
    db,
    kvb,
    mem_v,
    packs,
    mask_s,
    att_s,
    dq_s,
    gkv_s,
    gx_s,
    gx,
    gate_s,
    gate_m,
    gate_d,
    send_sem,
    recv_sem,
    local_sem,
):
    me = lax.axis_index("mem")
    dp = lax.axis_index("dp")
    x = me // 2
    c = me % 2
    o = 1 - c
    mate = 2 * x + o
    far = 2 * (1 - x)
    bf = jnp.bfloat16

    def remote(src, dst, send_k, recv_k, device):
        return pltpu.make_async_remote_copy(
            src_ref=src,
            dst_ref=dst,
            send_sem=send_sem.at[send_k],
            recv_sem=recv_sem.at[recv_k],
            device_id=device,
            device_id_type=MESH_ID,
        )

    def lanes(first, count):
        return pl.ds(pl.multiple_of(first * HD, HD), count * HD)

    barrier = pltpu.get_barrier_semaphore()
    for k in range(1, 4):
        pl.semaphore_signal(
            barrier, inc=1, device_id={"mem": (me + k) % 4}, device_id_type=MESH_ID
        )
    for k in range(1, n_dp):
        pl.semaphore_signal(
            barrier, inc=1, device_id={"dp": (dp + k) % n_dp}, device_id_type=MESH_ID
        )

    locals_ = [
        pltpu.make_async_copy(q_ref.at[:, lanes(c * HG, HG)], qb.at[c], local_sem.at[0]),
        pltpu.make_async_copy(d_ref.at[:, lanes(c * HG, HG)], db.at[c], local_sem.at[1]),
        pltpu.make_async_copy(kv_ref.at[pl.ds(c * HG, HG)], kvb.at[me], local_sem.at[2]),
        pltpu.make_async_copy(mem_ref, mem_v, local_sem.at[3]),
    ]
    for copy in locals_:
        copy.start()

    slots = 2 * 4

    def stored_flags(index):
        flags = []
        for low in range(2):
            block = jnp.int32(0)
            for r in range(slots):
                block = jnp.where(home_ref[0, r] == 2 * index + low, r, block)
            seen = block < limit_ref[0, 0]
            for h in range(H):
                found = ids_ref[0, 0, h, 0] == block
                for j in range(1, slots):
                    found = found | (ids_ref[0, 0, h, j] == block)
                flags.append(jnp.where(found & seen, 1, 0))
        return flags

    def places(flags):
        count = jnp.int32(0)
        result = []
        for flag in flags:
            result.append(count)
            count = count + flag
        return result

    mine = stored_flags(me)
    mine_at = places(mine)
    chosen = []
    for k in range(CAP):
        entry = jnp.int32(0)
        for e in range(2 * H):
            entry = jnp.where((mine[e] == 1) & (mine_at[e] == k), e, entry)
        chosen.append(entry)
    locals_[3].wait()
    for k in range(CAP):
        packs[me, k] = mem_v[chosen[k]]

    pl.semaphore_wait(barrier, 2 + n_dp)

    core_copies = [
        remote(q_ref.at[:, lanes(o * HG, HG)], qb.at[c], 0, 0, {"mem": mate}),
        remote(d_ref.at[:, lanes(o * HG, HG)], db.at[c], 1, 1, {"mem": mate}),
        remote(kv_ref.at[pl.ds(o * HG, HG)], kvb.at[me], 2, 2, {"mem": mate}),
        remote(packs.at[me], packs.at[me], 3, 3, {"mem": mate}),
    ]

    def kv_copy(to, hh):
        return remote(
            kv_ref.at[to * HG + hh],
            kvb.at[me, hh],
            4 + to * HG + hh,
            4 + c * HG + hh,
            {"mem": far + to},
        )

    pack_copy = remote(packs.at[me], packs.at[me], 12, 12, {"mem": far + c})
    pack_copy.start()

    @pl.when(x == 0)
    def _():
        for hh in range(HG):
            for to in range(2):
                kv_copy(to, hh).start()

    for copy in core_copies:
        copy.start()

    key_slot = lax.broadcasted_iota(jnp.int32, (H, slots * 64), 1) // 64
    block_of = jnp.zeros((H, slots * 64), jnp.int32)
    for r in range(slots):
        block_of = jnp.where(key_slot == home_ref[0, r], r, block_of)
    named = jnp.zeros((H, slots * 64), jnp.bool_)
    for j in range(slots):
        named = named | (block_of == lists_ref[0, 0, :, j : j + 1])
    mask_s[...] = jnp.where(named & (block_of < limit_ref[0, 0]), 0.0, neg_large)
    gate_s[...] = jnp.zeros_like(gate_s)

    def res_copy(kind, hh):
        head = c * HG + hh
        if kind == 0:
            return remote(
                att_s.at[o, hh], att_ref.at[:, lanes(head, 1)], 20 + hh, 20 + hh, {"mem": mate}
            )
        if kind == 1:
            return remote(
                dq_s.at[o, hh], dq_ref.at[:, lanes(head, 1)], 24 + hh, 24 + hh, {"mem": mate}
            )
        return remote(gkv_s.at[o, hh], gkv_ref.at[head], 28 + hh, 28 + hh, {"mem": mate})

    def gx_copy(to, hh):
        return remote(
            gx_s.at[to, hh],
            gx.at[c * HG + hh],
            32 + to * HG + hh,
            32 + c * HG + hh,
            {"mem": far + to},
        )

    def own_copy(kind, hh):
        head = c * HG + hh
        sem = local_sem.at[4 + kind * HG + hh]
        if kind == 0:
            return pltpu.make_async_copy(att_s.at[c, hh], att_ref.at[:, lanes(head, 1)], sem)
        if kind == 1:
            return pltpu.make_async_copy(dq_s.at[c, hh], dq_ref.at[:, lanes(head, 1)], sem)
        return pltpu.make_async_copy(gkv_s.at[c, hh], gkv_ref.at[head], sem)

    at = []
    for index in range(4):
        at.append([jnp.minimum(place, CAP - 1) for place in places(stored_flags(index))])

    def entry_place(index, low, hh):
        return jnp.where(c == 0, at[index][low * H + hh], at[index][low * H + HG + hh])

    for copy in locals_[:3]:
        copy.wait()
    for copy in core_copies:
        copy.wait_recv()
    pack_copy_in = remote(packs.at[me], packs.at[far + c], 12, 12, {"mem": mate})
    pack_copy_in.wait_recv()
    forward = remote(packs.at[far + c], packs.at[far + c], 13, 13, {"mem": mate})
    forward.start()
    remote(packs.at[me], packs.at[far + o], 13, 13, {"mem": mate}).wait_recv()

    gate_mem = [
        remote(gate_s, gate_m.at[k - 1], 40 + k, 40 + k, {"mem": (me + k) % 4})
        for k in range(1, 4)
    ]
    gate_dp = [
        remote(gate_d.at[0], gate_d.at[k], 43 + k, 43 + k, {"dp": (dp + k) % n_dp})
        for k in range(1, n_dp)
    ]

    def gate_step():
        for copy in gate_mem:
            copy.wait()
        gate_d[0] = gate_s[...] + gate_m[0] + gate_m[1] + gate_m[2]
        for copy in gate_dp:
            copy.start()

    def one_head(hh, later):
        rows = 2 * TOK_DEV
        keys_n = 2 * TOK_DEV * (1 + later)
        head = c * HG + hh
        query = qb[:, :, hh * HD : (hh + 1) * HD].reshape(rows, HD)
        dout = db[:, :, hh * HD : (hh + 1) * HD].reshape(rows, HD).astype(jnp.float32)
        gate = 1.0 / (1.0 + jnp.exp(-jnp.full((1, HD), bias_ref[head], jnp.float32)))
        mem_cot = gate * dout
        near_cot = (1.0 - gate) * dout
        near_cot16 = near_cot.astype(bf)

        entries = [
            packs[index, entry_place(index, low, hh)] for index in range(4) for low in range(2)
        ]
        mem_keys = jnp.concatenate([entry[0] for entry in entries], axis=0)
        mem_vals = jnp.concatenate([entry[1] for entry in entries], axis=0)
        mem_probs = probs_of(dot_nt(query, mem_keys) * SCALE + mask_s[pl.ds(head, 1), :])
        mem_out = dot_nn(mem_probs.astype(bf), mem_vals)
        mem_delta = jnp.sum(mem_cot * mem_out, axis=1, keepdims=True)
        mem_ds = (
            mem_probs * ((dot_nt(mem_cot.astype(bf), mem_vals) - mem_delta) * SCALE)
        ).astype(bf)
        query_grad = dot_nn(mem_ds, mem_keys)

        if later:
            for frm in range(2):
                remote(
                    kv_ref.at[0], kvb.at[frm, hh], 0, 4 + frm * HG + hh, {"mem": mate}
                ).wait_recv()
            near_keys = kvb[:, hh, 0].reshape(keys_n, HD)
            near_vals = kvb[:, hh, 1].reshape(keys_n, HD)
        else:
            near_keys = kvb[0:2, hh, 0].reshape(keys_n, HD)
            near_vals = kvb[0:2, hh, 1].reshape(keys_n, HD)
        row = lax.broadcasted_iota(jnp.int32, (rows, keys_n), 0)
        col = lax.broadcasted_iota(jnp.int32, (rows, keys_n), 1)
        causal = col <= row + (keys_n - rows)
        near_probs = probs_of(
            jnp.where(causal, dot_nt(query, near_keys) * SCALE, neg_large)
        )
        near_low = near_probs.astype(bf)
        near_out = dot_nn(near_low, near_vals)
        gate_s[pl.ds(head, 1), :] = (
            jnp.sum(dout * (mem_out - near_out), axis=0, keepdims=True) * gate * (1.0 - gate)
        )
        if hh == HG - 1:
            for copy in gate_mem:
                copy.start()
        near_delta = jnp.sum(near_cot * near_out, axis=1, keepdims=True)
        near_ds = (
            near_probs * ((dot_nt(near_cot16, near_vals) - near_delta) * SCALE)
        ).astype(bf)
        key_grad = dot_tn(near_ds, query).astype(bf)
        val_grad = dot_tn(near_low, near_cot16).astype(bf)
        split = keys_n - rows
        if later:
            gx_s[:, hh, 0] = key_grad[:split].reshape(2, TOK_DEV, HD)
            gx_s[:, hh, 1] = val_grad[:split].reshape(2, TOK_DEV, HD)
            for to in range(2):
                gx_copy(to, hh).start()
        gkv_s[:, hh, 0] = key_grad[split:].reshape(2, TOK_DEV, HD)
        gkv_s[:, hh, 1] = val_grad[split:].reshape(2, TOK_DEV, HD)
        mixed = (gate * mem_out + (1.0 - gate) * near_out).astype(bf)
        att_s[:, hh] = mixed.reshape(2, TOK_DEV, HD)
        if later and hh == HG - 1:
            gate_step()
        query_grad = query_grad + dot_nn(near_ds, near_keys)
        dq_s[:, hh] = query_grad.astype(bf).reshape(2, TOK_DEV, HD)
        for kind in range(3):
            res_copy(kind, hh).start()
            own_copy(kind, hh).start()

    @pl.when(x == 0)
    def _():
        for hh in range(HG):
            one_head(hh, False)
        gate_step()

    @pl.when(x == 1)
    def _():
        for hh in range(HG):
            one_head(hh, True)

    for kind in range(3):
        for hh in range(HG):
            own_copy(kind, hh).wait()
            copy = res_copy(kind, hh)
            copy.wait_send()
    for hh in range(HG):
        other = o * HG + hh
        remote(
            att_s.at[0, 0], att_ref.at[:, lanes(other, 1)], 0, 20 + hh, {"mem": mate}
        ).wait_recv()
        remote(
            dq_s.at[0, 0], dq_ref.at[:, lanes(other, 1)], 0, 24 + hh, {"mem": mate}
        ).wait_recv()
        remote(gkv_s.at[0, 0], gkv_ref.at[other], 0, 28 + hh, {"mem": mate}).wait_recv()

    @pl.when(x == 0)
    def _():
        for hh in range(HG):
            for to in range(2):
                kv_copy(to, hh).wait_send()
        for hh in range(HG):
            for frm in range(2):
                head = frm * HG + hh
                remote(
                    gkv_s.at[0, 0], gx.at[head], 0, 32 + head, {"mem": mate}
                ).wait_recv()
                gkv_ref[head] = (
                    gkv_ref[head].astype(jnp.float32) + gx[head].astype(jnp.float32)
                ).astype(bf)

    @pl.when(x == 1)
    def _():
        for hh in range(HG):
            for to in range(2):
                gx_copy(to, hh).wait_send()

    pack_copy.wait_send()
    forward.wait_send()
    for copy in core_copies:
        copy.wait_send()
    for copy in gate_dp:
        copy.wait()
    total = gate_d[0]
    for k in range(1, n_dp):
        total = total + gate_d[k]
    summed = jnp.broadcast_to(jnp.sum(total, axis=1, keepdims=True), (H, HD))
    eye = lax.broadcasted_iota(jnp.int32, (H, HD), 0) == lax.broadcasted_iota(
        jnp.int32, (H, HD), 1
    )
    gate_ref[...] = jnp.sum(jnp.where(eye, summed, 0.0), axis=0, keepdims=True)


def one_stretch_per_document(
    n_dp, queries, local_kv, memory_kv, block_home, retrieved, stretch_pos, gate_bias, d_out
):
    bf = jnp.bfloat16
    kv_heads = jnp.transpose(local_kv.reshape(TOK_DEV, 2, H, HD), (2, 1, 0, 3))
    vmem = pl.BlockSpec(memory_space=pltpu.VMEM)
    smem = pl.BlockSpec(memory_space=pltpu.SMEM)
    hbm = pl.BlockSpec(memory_space=pl.ANY)
    n_sems = 44 + n_dp
    attended, grad_queries, grad_kv, grad_gate = pl.pallas_call(
        functools.partial(layer_kernel, n_dp),
        out_shape=(
            jax.ShapeDtypeStruct((TOK_DEV, H * HD), bf),
            jax.ShapeDtypeStruct((TOK_DEV, H * HD), bf),
            jax.ShapeDtypeStruct((H, 2, TOK_DEV, HD), bf),
            jax.ShapeDtypeStruct((1, HD), jnp.float32),
        ),
        in_specs=[hbm, hbm, vmem, hbm, smem, vmem, smem, smem, smem],
        out_specs=(vmem, vmem, vmem, vmem),
        scratch_shapes=[
            pltpu.VMEM((2, TOK_DEV, HG * HD), bf),
            pltpu.VMEM((2, TOK_DEV, HG * HD), bf),
            pltpu.VMEM((4, HG, 2, TOK_DEV, HD), bf),
            pltpu.VMEM((2 * H, 2, 64, HD), bf),
            pltpu.VMEM((4, CAP, 2, 64, HD), bf),
            pltpu.VMEM((H, 512), jnp.float32),
            pltpu.VMEM((2, HG, TOK_DEV, HD), bf),
            pltpu.VMEM((2, HG, TOK_DEV, HD), bf),
            pltpu.VMEM((2, HG, 2, TOK_DEV, HD), bf),
            pltpu.VMEM((2, HG, 2, TOK_DEV, HD), bf),
            pltpu.VMEM((H, 2, TOK_DEV, HD), bf),
            pltpu.VMEM((H, HD), jnp.float32),
            pltpu.VMEM((3, H, HD), jnp.float32),
            pltpu.VMEM((n_dp, H, HD), jnp.float32),
            pltpu.SemaphoreType.DMA((n_sems,)),
            pltpu.SemaphoreType.DMA((n_sems,)),
            pltpu.SemaphoreType.DMA((4 + 3 * HG,)),
        ],
        compiler_params=pltpu.CompilerParams(
            collective_id=0, has_side_effects=True, vmem_limit_bytes=40 * 1024 * 1024
        ),
    )(
        queries[0],
        d_out[0],
        kv_heads,
        memory_kv[0].reshape(2 * H, 2, 64, HD),
        block_home,
        retrieved,
        retrieved,
        stretch_pos,
        gate_bias,
    )
    grad_kv = jnp.transpose(grad_kv, (2, 1, 0, 3)).reshape(1, TOK_DEV, 2, H * HD)
    return (attended[None], grad_queries[None], grad_kv, grad_gate[0, :H])


def solution(mesh):
    body = per_device
    if mesh.shape["mem"] == STRETCH // TOK_DEV:
        body = functools.partial(one_stretch_per_document, mesh.shape["dp"])
    in_specs = (
        P(("groups", "dp"), "mem", None),
        P(("groups", "dp"), "mem", None, None),
        P(("groups", "dp"), "mem", None, None, None, None),
        P(("groups", "dp"), None),
        P(("groups", "dp"), None, None, None),
        P(("groups", "dp"), None),
        P(),
        P(("groups", "dp"), "mem", None),
    )
    out_specs = (
        P(("groups", "dp"), "mem", None),
        P(("groups", "dp"), "mem", None),
        P(("groups", "dp"), "mem", None, None),
        P("groups"),
    )
    return jax.shard_map(
        body, mesh=mesh, in_specs=in_specs, out_specs=out_specs, check_vma=False
    )
```

```python
import functools

import jax
import jax.numpy as jnp
from jax import lax
from jax.experimental import pallas as pl
from jax.experimental.pallas import tpu as pltpu
from jax.sharding import PartitionSpec as P

H = 8
HD = 128
TOK_DEV = 128
STRETCH = 512


neg_large = -1e30


def from_partner(block, axis, stride):
    count = lax.axis_size(axis)
    route = []
    for low in range(count):
        high = low | 1 << stride
        if high != low and high < count:
            route += [(low, high), (high, low)]
    return lax.ppermute(block, axis, route)


def masked_softmax(scores, visible):
    scores = jnp.where(visible, scores, neg_large)
    row_top = jnp.max(scores, axis=-1, keepdims=True)
    lifted = jnp.exp(scores - row_top)
    row_total = jnp.sum(lifted, axis=-1, keepdims=True)
    return lax.optimization_barrier((lifted / row_total).astype(jnp.bfloat16))


def fetch_blocks(memory_kv, slot_ids, head_ids):
    everything = lax.all_gather(memory_kv, "mem", axis=1, tiled=True)[0]
    return everything[slot_ids, head_ids]


def attend(query_heads, cotangent, fetched, visible, near_keys, near_vals, near_mask, gate_value):
    inv_sqrt = HD ** (-0.5)
    heads_here = fetched.shape[0]
    keys_n = fetched.shape[1] * fetched.shape[3]
    mem_keys = fetched[:, :, 0].reshape(heads_here, keys_n, HD)
    mem_vals = fetched[:, :, 1].reshape(heads_here, keys_n, HD)
    mem_mask = jnp.repeat(visible, fetched.shape[3], axis=1)[:, None, :]
    mem_scores = (
        jnp.einsum("qhd,hkd->hqk", query_heads, mem_keys, preferred_element_type=jnp.float32)
        * inv_sqrt
    )
    mem_probs = masked_softmax(mem_scores, mem_mask)
    mem_out = jnp.einsum("hqk,hkd->qhd", mem_probs, mem_vals, preferred_element_type=jnp.float32)
    near_scores = (
        jnp.einsum("qhd,khd->hqk", query_heads, near_keys, preferred_element_type=jnp.float32)
        * inv_sqrt
    )
    near_probs = masked_softmax(near_scores, near_mask)
    near_out = jnp.einsum("hqk,khd->qhd", near_probs, near_vals, preferred_element_type=jnp.float32)
    gate_col = gate_value[None, :, None]
    mixed = gate_col * mem_out + (1.0 - gate_col) * near_out
    mem_grad_out = gate_col * cotangent
    near_grad_out = (1.0 - gate_col) * cotangent
    gate_terms = (
        jnp.sum(cotangent * (mem_out - near_out), axis=(0, 2)) * gate_value * (1.0 - gate_value)
    )
    mem_delta = jnp.transpose(jnp.sum(mem_grad_out * mem_out, axis=2))[:, :, None]
    near_delta = jnp.transpose(jnp.sum(near_grad_out * near_out, axis=2))[:, :, None]
    mem_grad_low = mem_grad_out.astype(jnp.bfloat16)
    near_grad_low = near_grad_out.astype(jnp.bfloat16)
    mem_dprobs = jnp.einsum(
        "qhd,hkd->hqk", mem_grad_low, mem_vals, preferred_element_type=jnp.float32
    )
    mem_dscores = (mem_probs.astype(jnp.float32) * (mem_dprobs - mem_delta) * inv_sqrt).astype(
        jnp.bfloat16
    )
    near_dprobs = jnp.einsum(
        "qhd,khd->hqk", near_grad_low, near_vals, preferred_element_type=jnp.float32
    )
    near_dscores = (near_probs.astype(jnp.float32) * (near_dprobs - near_delta) * inv_sqrt).astype(
        jnp.bfloat16
    )
    query_grad = jnp.einsum(
        "hqk,hkd->qhd", mem_dscores, mem_keys, preferred_element_type=jnp.float32
    )
    query_grad = query_grad + jnp.einsum(
        "hqk,khd->qhd", near_dscores, near_keys, preferred_element_type=jnp.float32
    )
    return (mixed, query_grad, near_dscores, near_probs, near_grad_low, gate_terms)


def regroup(pieces):
    piece_count = pieces.shape[0]
    for bit_number in range(piece_count.bit_length() - 1):
        moving_rows = jnp.asarray(
            [k for k in range(piece_count) if k >> bit_number & 1], dtype=jnp.int32
        )
        arrived = from_partner(pieces[moving_rows], "mem", bit_number)
        pieces = pieces.at[moving_rows].set(arrived)
    return pieces


def per_device(queries, local_kv, memory_kv, block_home, retrieved, stretch_pos, gate_bias, d_out):
    my_index = lax.axis_index("mem")
    per_stretch = STRETCH // TOK_DEV
    rank_in_span = my_index % per_stretch
    stretch_index = my_index // per_stretch
    block_ids_all = lax.dynamic_index_in_dim(retrieved[0], stretch_index, 0, keepdims=False)
    stretch_limit = lax.dynamic_index_in_dim(stretch_pos[0], stretch_index, 0, keepdims=False)
    gate_value = jax.nn.sigmoid(gate_bias)
    head_group = H // per_stretch
    rank_order = rank_in_span ^ jnp.arange(per_stretch, dtype=jnp.int32)
    packed = jnp.concatenate(
        [
            queries[0].reshape(TOK_DEV, 1, H, HD),
            local_kv[0].reshape(TOK_DEV, 2, H, HD),
            d_out[0].reshape(TOK_DEV, 1, H, HD),
        ],
        axis=1,
    )
    by_rank = jnp.transpose(
        packed.reshape(TOK_DEV, 4, per_stretch, head_group, HD), (2, 0, 1, 3, 4)
    )
    gathered = regroup(by_rank[rank_order])[rank_order].reshape(STRETCH, 4, head_group, HD)
    query_heads = gathered[:, 0]
    first_head = rank_in_span * head_group
    head_ids = (first_head + jnp.arange(head_group, dtype=jnp.int32))[:, None]
    block_ids = lax.dynamic_slice_in_dim(block_ids_all, first_head, head_group, 0)
    visible = (block_ids >= 0) & (block_ids < stretch_limit)
    slot_ids = block_home[0][jnp.clip(block_ids, 0, block_home.shape[1] - 1)]
    fetched = fetch_blocks(memory_kv, slot_ids, head_ids)
    positions = jnp.arange(STRETCH, dtype=jnp.int32)
    near_mask = (positions[None, :] <= positions[:, None])[None]
    gate_mine = lax.dynamic_slice_in_dim(gate_value, first_head, head_group, 0)
    cotangent = gathered[:, 3].astype(jnp.float32)
    mixed, query_grad, near_dscores, near_probs, near_grad_low, gate_terms = attend(
        query_heads,
        cotangent,
        fetched,
        visible,
        gathered[:, 1],
        gathered[:, 2],
        near_mask,
        gate_mine,
    )
    ds_blocks = near_dscores.reshape(head_group, per_stretch, TOK_DEV, STRETCH)
    probs_blocks = near_probs.reshape(head_group, per_stretch, TOK_DEV, STRETCH)
    query_blocks = query_heads.reshape(per_stretch, TOK_DEV, head_group, HD)
    cot_blocks = near_grad_low.reshape(per_stretch, TOK_DEV, head_group, HD)
    key_terms = jnp.einsum(
        "hbqk,bqhd->bkhd", ds_blocks, query_blocks, preferred_element_type=jnp.float32
    ).astype(jnp.bfloat16)
    value_terms = jnp.einsum(
        "hbqk,bqhd->bkhd", probs_blocks, cot_blocks, preferred_element_type=jnp.float32
    ).astype(jnp.bfloat16)
    key_grad = jnp.sum(key_terms.astype(jnp.float32), axis=0).astype(jnp.bfloat16)
    value_grad = jnp.sum(value_terms.astype(jnp.float32), axis=0).astype(jnp.bfloat16)
    outgoing = jnp.stack(
        [mixed.astype(jnp.bfloat16), query_grad.astype(jnp.bfloat16), key_grad, value_grad], axis=1
    )
    outgoing = outgoing.reshape(per_stretch, TOK_DEV, 4, head_group, HD)
    returned = regroup(outgoing[rank_order])[rank_order]
    results = jnp.transpose(returned, (1, 2, 0, 3, 4)).reshape(TOK_DEV, 4, H * HD)
    attended = results[:, 0][None]
    grad_queries = results[:, 1][None]
    grad_kv = results[:, 2:4][None]
    gate_full = lax.dynamic_update_slice_in_dim(
        jnp.zeros((H,), jnp.float32), gate_terms, first_head, 0
    )
    grad_gate = lax.psum(gate_full, ("mem", "dp"))
    return (attended, grad_queries, grad_kv, grad_gate)


MESH_ID = pl.DeviceIdType.MESH
SCALE = HD ** (-0.5)
CAP = 8
HG = H // 2


def dot_nt(a, b):
    return lax.dot_general(a, b, (((1,), (1,)), ((), ())), preferred_element_type=jnp.float32)


def dot_tn(a, b):
    return lax.dot_general(a, b, (((0,), (0,)), ((), ())), preferred_element_type=jnp.float32)


def dot_nn(a, b):
    return jnp.dot(a, b, preferred_element_type=jnp.float32)


def probs_of(scores):
    top = jnp.max(scores, axis=1, keepdims=True)
    lifted = jnp.exp(scores - top)
    return lifted * (1.0 / jnp.sum(lifted, axis=1, keepdims=True))


def layer_kernel(
    n_dp,
    q_ref,
    d_ref,
    kv_ref,
    mem_ref,
    home_ref,
    lists_ref,
    ids_ref,
    limit_ref,
    bias_ref,
    att_ref,
    dq_ref,
    gint_ref,
    gate_ref,
    gkv_v,
    qb,
    db,
    kvb,
    mem_v,
    packs,
    mask_s,
    att_s,
    dq_s,
    gkv_s,
    gx_s,
    gx,
    gate_s,
    gate_m,
    gate_d,
    send_sem,
    recv_sem,
    local_sem,
):
    me = lax.axis_index("mem")
    dp = lax.axis_index("dp")
    x = me // 2
    c = me % 2
    o = 1 - c
    mate = 2 * x + o
    far = 2 * (1 - x)
    bf = jnp.bfloat16

    def remote(src, dst, send_k, recv_k, device):
        return pltpu.make_async_remote_copy(
            src_ref=src,
            dst_ref=dst,
            send_sem=send_sem.at[send_k],
            recv_sem=recv_sem.at[recv_k],
            device_id=device,
            device_id_type=MESH_ID,
        )

    def lanes(first, count):
        return pl.ds(pl.multiple_of(first * HD, HD), count * HD)

    barrier = pltpu.get_barrier_semaphore()
    for k in range(1, 4):
        pl.semaphore_signal(
            barrier, inc=1, device_id={"mem": (me + k) % 4}, device_id_type=MESH_ID
        )
    for k in range(1, n_dp):
        pl.semaphore_signal(
            barrier, inc=1, device_id={"dp": (dp + k) % n_dp}, device_id_type=MESH_ID
        )

    locals_ = [
        pltpu.make_async_copy(q_ref.at[:, lanes(c * HG, HG)], qb.at[c], local_sem.at[0]),
        pltpu.make_async_copy(d_ref.at[:, lanes(c * HG, HG)], db.at[c], local_sem.at[1]),
        pltpu.make_async_copy(kv_ref.at[pl.ds(c * HG, HG)], kvb.at[me], local_sem.at[2]),
        pltpu.make_async_copy(mem_ref, mem_v, local_sem.at[3]),
    ]
    for copy in locals_:
        copy.start()

    slots = 2 * 4

    def stored_flags(index):
        flags = []
        for low in range(2):
            block = jnp.int32(0)
            for r in range(slots):
                block = jnp.where(home_ref[0, r] == 2 * index + low, r, block)
            seen = block < limit_ref[0, 0]
            for h in range(H):
                found = ids_ref[0, 0, h, 0] == block
                for j in range(1, slots):
                    found = found | (ids_ref[0, 0, h, j] == block)
                flags.append(jnp.where(found & seen, 1, 0))
        return flags

    def places(flags):
        count = jnp.int32(0)
        result = []
        for flag in flags:
            result.append(count)
            count = count + flag
        return result

    mine = stored_flags(me)
    mine_at = places(mine)
    chosen = []
    for k in range(CAP):
        entry = jnp.int32(0)
        for e in range(2 * H):
            entry = jnp.where((mine[e] == 1) & (mine_at[e] == k), e, entry)
        chosen.append(entry)
    locals_[3].wait()
    for k in range(CAP):
        packs[me, k] = mem_v[chosen[k]]

    pl.semaphore_wait(barrier, 2 + n_dp)

    core_copies = [
        remote(q_ref.at[:, lanes(o * HG, HG)], qb.at[c], 0, 0, {"mem": mate}),
        remote(d_ref.at[:, lanes(o * HG, HG)], db.at[c], 1, 1, {"mem": mate}),
        remote(kv_ref.at[pl.ds(o * HG, HG)], kvb.at[me], 2, 2, {"mem": mate}),
        remote(packs.at[me], packs.at[me], 3, 3, {"mem": mate}),
    ]

    def kv_copy(to, hh):
        return remote(
            kv_ref.at[to * HG + hh],
            kvb.at[me, hh],
            4 + to * HG + hh,
            4 + c * HG + hh,
            {"mem": far + to},
        )

    for copy in core_copies[:3]:
        copy.start()
    pack_copy = remote(packs.at[me], packs.at[me], 12, 12, {"mem": far + c})
    pack_copy.start()

    @pl.when(x == 0)
    def _():
        for hh in range(HG):
            for to in range(2):
                kv_copy(to, hh).start()

    core_copies[3].start()

    key_slot = lax.broadcasted_iota(jnp.int32, (H, slots * 64), 1) // 64
    block_of = jnp.zeros((H, slots * 64), jnp.int32)
    for r in range(slots):
        block_of = jnp.where(key_slot == home_ref[0, r], r, block_of)
    named = jnp.zeros((H, slots * 64), jnp.bool_)
    for j in range(slots):
        named = named | (block_of == lists_ref[0, 0, :, j : j + 1])
    mask_s[...] = jnp.where(named & (block_of < limit_ref[0, 0]), 0.0, neg_large)
    gate_s[...] = jnp.zeros_like(gate_s)

    def res_copy(kind, hh):
        head = c * HG + hh
        if kind == 0:
            return remote(
                att_s.at[o, hh], att_ref.at[:, lanes(head, 1)], 20 + hh, 20 + hh, {"mem": mate}
            )
        if kind == 1:
            return remote(
                dq_s.at[o, hh], dq_ref.at[:, lanes(head, 1)], 24 + hh, 24 + hh, {"mem": mate}
            )
        return remote(gkv_s.at[o, hh], gkv_v.at[head], 28 + hh, 28 + hh, {"mem": mate})

    def gx_copy(to, hh):
        return remote(
            gx_s.at[to, hh],
            gx.at[c * HG + hh],
            32 + to * HG + hh,
            32 + c * HG + hh,
            {"mem": far + to},
        )

    def own_copy(kind, hh):
        head = c * HG + hh
        sem = local_sem.at[4 + kind * HG + hh]
        if kind == 0:
            return pltpu.make_async_copy(att_s.at[c, hh], att_ref.at[:, lanes(head, 1)], sem)
        if kind == 1:
            return pltpu.make_async_copy(dq_s.at[c, hh], dq_ref.at[:, lanes(head, 1)], sem)
        return pltpu.make_async_copy(gkv_s.at[c, hh], gkv_v.at[head], sem)

    at = []
    for index in range(4):
        at.append([jnp.minimum(place, CAP - 1) for place in places(stored_flags(index))])

    def entry_place(index, low, hh):
        return jnp.where(c == 0, at[index][low * H + hh], at[index][low * H + HG + hh])

    for copy in locals_[:3]:
        copy.wait()
    for copy in core_copies:
        copy.wait_recv()
    pack_copy_in = remote(packs.at[me], packs.at[far + c], 12, 12, {"mem": mate})
    pack_copy_in.wait_recv()
    forward = remote(packs.at[far + c], packs.at[far + c], 13, 13, {"mem": mate})
    forward.start()
    remote(packs.at[me], packs.at[far + o], 13, 13, {"mem": mate}).wait_recv()

    gate_mem = [
        remote(gate_s, gate_m.at[k - 1], 40 + k, 40 + k, {"mem": (me + k) % 4})
        for k in range(1, 4)
    ]
    gate_dp = [
        remote(gate_d.at[0], gate_d.at[k], 43 + k, 43 + k, {"dp": (dp + k) % n_dp})
        for k in range(1, n_dp)
    ]

    def gate_step():
        for copy in gate_mem:
            copy.wait()
        gate_d[0] = gate_s[...] + gate_m[0] + gate_m[1] + gate_m[2]
        for copy in gate_dp:
            copy.start()

    def one_head(hh, later):
        rows = 2 * TOK_DEV
        keys_n = 2 * TOK_DEV * (1 + later)
        head = c * HG + hh
        query = qb[:, :, hh * HD : (hh + 1) * HD].reshape(rows, HD)
        dout = db[:, :, hh * HD : (hh + 1) * HD].reshape(rows, HD).astype(jnp.float32)
        gate = 1.0 / (1.0 + jnp.exp(-jnp.full((1, HD), bias_ref[head], jnp.float32)))
        mem_cot = gate * dout
        near_cot = (1.0 - gate) * dout
        near_cot16 = near_cot.astype(bf)

        entries = [
            packs[index, entry_place(index, low, hh)] for index in range(4) for low in range(2)
        ]
        mem_keys = jnp.concatenate([entry[0] for entry in entries], axis=0)
        mem_vals = jnp.concatenate([entry[1] for entry in entries], axis=0)
        mem_probs = probs_of(dot_nt(query, mem_keys) * SCALE + mask_s[pl.ds(head, 1), :])
        mem_out = dot_nn(mem_probs.astype(bf), mem_vals)
        mem_delta = jnp.sum(mem_cot * mem_out, axis=1, keepdims=True)
        mem_ds = (
            mem_probs * ((dot_nt(mem_cot.astype(bf), mem_vals) - mem_delta) * SCALE)
        ).astype(bf)
        query_grad = dot_nn(mem_ds, mem_keys)

        if later:
            for frm in range(2):
                remote(
                    kv_ref.at[0], kvb.at[frm, hh], 0, 4 + frm * HG + hh, {"mem": mate}
                ).wait_recv()
            near_keys = kvb[:, hh, 0].reshape(keys_n, HD)
            near_vals = kvb[:, hh, 1].reshape(keys_n, HD)
        else:
            near_keys = kvb[0:2, hh, 0].reshape(keys_n, HD)
            near_vals = kvb[0:2, hh, 1].reshape(keys_n, HD)
        row = lax.broadcasted_iota(jnp.int32, (rows, keys_n), 0)
        col = lax.broadcasted_iota(jnp.int32, (rows, keys_n), 1)
        causal = col <= row + (keys_n - rows)
        near_probs = probs_of(
            jnp.where(causal, dot_nt(query, near_keys) * SCALE, neg_large)
        )
        near_low = near_probs.astype(bf)
        near_out = dot_nn(near_low, near_vals)
        gate_s[pl.ds(head, 1), :] = (
            jnp.sum(dout * (mem_out - near_out), axis=0, keepdims=True) * gate * (1.0 - gate)
        )
        if hh == HG - 1:
            for copy in gate_mem:
                copy.start()
        near_delta = jnp.sum(near_cot * near_out, axis=1, keepdims=True)
        near_ds = (
            near_probs * ((dot_nt(near_cot16, near_vals) - near_delta) * SCALE)
        ).astype(bf)
        key_grad = dot_tn(near_ds, query).astype(bf)
        val_grad = dot_tn(near_low, near_cot16).astype(bf)
        split = keys_n - rows
        if later:
            gx_s[:, hh, 0] = key_grad[:split].reshape(2, TOK_DEV, HD)
            gx_s[:, hh, 1] = val_grad[:split].reshape(2, TOK_DEV, HD)
            for to in range(2):
                gx_copy(to, hh).start()
        gkv_s[:, hh, 0] = key_grad[split:].reshape(2, TOK_DEV, HD)
        gkv_s[:, hh, 1] = val_grad[split:].reshape(2, TOK_DEV, HD)
        mixed = (gate * mem_out + (1.0 - gate) * near_out).astype(bf)
        att_s[:, hh] = mixed.reshape(2, TOK_DEV, HD)
        if later and hh == HG - 1:
            gate_step()
        query_grad = query_grad + dot_nn(near_ds, near_keys)
        dq_s[:, hh] = query_grad.astype(bf).reshape(2, TOK_DEV, HD)
        for kind in range(3):
            res_copy(kind, hh).start()
            own_copy(kind, hh).start()

    @pl.when(x == 0)
    def _():
        for hh in range(HG):
            one_head(hh, False)
        gate_step()

    @pl.when(x == 1)
    def _():
        for hh in range(HG):
            one_head(hh, True)

    for kind in range(3):
        for hh in range(HG):
            own_copy(kind, hh).wait()
            copy = res_copy(kind, hh)
            copy.wait_send()
    for hh in range(HG):
        other = o * HG + hh
        remote(
            att_s.at[0, 0], att_ref.at[:, lanes(other, 1)], 0, 20 + hh, {"mem": mate}
        ).wait_recv()
        remote(
            dq_s.at[0, 0], dq_ref.at[:, lanes(other, 1)], 0, 24 + hh, {"mem": mate}
        ).wait_recv()
        remote(gkv_s.at[0, 0], gkv_v.at[other], 0, 28 + hh, {"mem": mate}).wait_recv()

    def join_pairs(head, both):
        gint_ref[:, :, head * HD : (head + 1) * HD] = jnp.stack([both[0], both[1]], axis=1)

    @pl.when(x == 0)
    def _():
        for hh in range(HG):
            for to in range(2):
                kv_copy(to, hh).wait_send()
        for hh in range(HG):
            for frm in range(2):
                head = frm * HG + hh
                remote(
                    gkv_s.at[0, 0], gx.at[head], 0, 32 + head, {"mem": mate}
                ).wait_recv()
                both = gkv_v[head].astype(jnp.float32) + gx[head].astype(jnp.float32)
                join_pairs(head, both.astype(bf))

    @pl.when(x == 1)
    def _():
        for head in range(H):
            join_pairs(head, gkv_v[head])
        for hh in range(HG):
            for to in range(2):
                gx_copy(to, hh).wait_send()

    pack_copy.wait_send()
    forward.wait_send()
    for copy in core_copies:
        copy.wait_send()
    for copy in gate_dp:
        copy.wait()
    total = gate_d[0]
    for k in range(1, n_dp):
        total = total + gate_d[k]
    summed = jnp.broadcast_to(jnp.sum(total, axis=1, keepdims=True), (H, HD))
    eye = lax.broadcasted_iota(jnp.int32, (H, HD), 0) == lax.broadcasted_iota(
        jnp.int32, (H, HD), 1
    )
    gate_ref[...] = jnp.sum(jnp.where(eye, summed, 0.0), axis=0, keepdims=True)


def one_stretch_per_document(
    n_dp, queries, local_kv, memory_kv, block_home, retrieved, stretch_pos, gate_bias, d_out
):
    bf = jnp.bfloat16
    kv_heads = jnp.transpose(local_kv.reshape(TOK_DEV, 2, H, HD), (2, 1, 0, 3))
    vmem = pl.BlockSpec(memory_space=pltpu.VMEM)
    smem = pl.BlockSpec(memory_space=pltpu.SMEM)
    hbm = pl.BlockSpec(memory_space=pl.ANY)
    n_sems = 44 + n_dp
    attended, grad_queries, grad_kv, grad_gate = pl.pallas_call(
        functools.partial(layer_kernel, n_dp),
        out_shape=(
            jax.ShapeDtypeStruct((TOK_DEV, H * HD), bf),
            jax.ShapeDtypeStruct((TOK_DEV, H * HD), bf),
            jax.ShapeDtypeStruct((TOK_DEV, 2, H * HD), bf),
            jax.ShapeDtypeStruct((1, HD), jnp.float32),
        ),
        in_specs=[hbm, hbm, vmem, hbm, smem, vmem, smem, smem, smem],
        out_specs=(vmem, vmem, vmem, vmem),
        scratch_shapes=[
            pltpu.VMEM((H, 2, TOK_DEV, HD), bf),
            pltpu.VMEM((2, TOK_DEV, HG * HD), bf),
            pltpu.VMEM((2, TOK_DEV, HG * HD), bf),
            pltpu.VMEM((4, HG, 2, TOK_DEV, HD), bf),
            pltpu.VMEM((2 * H, 2, 64, HD), bf),
            pltpu.VMEM((4, CAP, 2, 64, HD), bf),
            pltpu.VMEM((H, 512), jnp.float32),
            pltpu.VMEM((2, HG, TOK_DEV, HD), bf),
            pltpu.VMEM((2, HG, TOK_DEV, HD), bf),
            pltpu.VMEM((2, HG, 2, TOK_DEV, HD), bf),
            pltpu.VMEM((2, HG, 2, TOK_DEV, HD), bf),
            pltpu.VMEM((H, 2, TOK_DEV, HD), bf),
            pltpu.VMEM((H, HD), jnp.float32),
            pltpu.VMEM((3, H, HD), jnp.float32),
            pltpu.VMEM((n_dp, H, HD), jnp.float32),
            pltpu.SemaphoreType.DMA((n_sems,)),
            pltpu.SemaphoreType.DMA((n_sems,)),
            pltpu.SemaphoreType.DMA((4 + 3 * HG,)),
        ],
        compiler_params=pltpu.CompilerParams(
            collective_id=0, has_side_effects=True, vmem_limit_bytes=40 * 1024 * 1024
        ),
    )(
        queries[0],
        d_out[0],
        kv_heads,
        memory_kv[0].reshape(2 * H, 2, 64, HD),
        block_home,
        retrieved,
        retrieved,
        stretch_pos,
        gate_bias,
    )
    return (attended[None], grad_queries[None], grad_kv[None], grad_gate[0, :H])


def solution(mesh):
    body = per_device
    if mesh.shape["mem"] == STRETCH // TOK_DEV:
        body = functools.partial(one_stretch_per_document, mesh.shape["dp"])
    in_specs = (
        P(("groups", "dp"), "mem", None),
        P(("groups", "dp"), "mem", None, None),
        P(("groups", "dp"), "mem", None, None, None, None),
        P(("groups", "dp"), None),
        P(("groups", "dp"), None, None, None),
        P(("groups", "dp"), None),
        P(),
        P(("groups", "dp"), "mem", None),
    )
    out_specs = (
        P(("groups", "dp"), "mem", None),
        P(("groups", "dp"), "mem", None),
        P(("groups", "dp"), "mem", None, None),
        P("groups"),
    )
    return jax.shard_map(
        body, mesh=mesh, in_specs=in_specs, out_specs=out_specs, check_vma=False
    )
```

```python
import functools

import jax
import jax.numpy as jnp
from jax import lax
from jax.experimental import pallas as pl
from jax.experimental.pallas import tpu as pltpu
from jax.sharding import PartitionSpec as P

H = 8
HD = 128
TOK_DEV = 128
STRETCH = 512


neg_large = -1e30


def from_partner(block, axis, stride):
    count = lax.axis_size(axis)
    route = []
    for low in range(count):
        high = low | 1 << stride
        if high != low and high < count:
            route += [(low, high), (high, low)]
    return lax.ppermute(block, axis, route)


def masked_softmax(scores, visible):
    scores = jnp.where(visible, scores, neg_large)
    row_top = jnp.max(scores, axis=-1, keepdims=True)
    lifted = jnp.exp(scores - row_top)
    row_total = jnp.sum(lifted, axis=-1, keepdims=True)
    return lax.optimization_barrier((lifted / row_total).astype(jnp.bfloat16))


def fetch_blocks(memory_kv, slot_ids, head_ids):
    everything = lax.all_gather(memory_kv, "mem", axis=1, tiled=True)[0]
    return everything[slot_ids, head_ids]


def attend(query_heads, cotangent, fetched, visible, near_keys, near_vals, near_mask, gate_value):
    inv_sqrt = HD ** (-0.5)
    heads_here = fetched.shape[0]
    keys_n = fetched.shape[1] * fetched.shape[3]
    mem_keys = fetched[:, :, 0].reshape(heads_here, keys_n, HD)
    mem_vals = fetched[:, :, 1].reshape(heads_here, keys_n, HD)
    mem_mask = jnp.repeat(visible, fetched.shape[3], axis=1)[:, None, :]
    mem_scores = (
        jnp.einsum("qhd,hkd->hqk", query_heads, mem_keys, preferred_element_type=jnp.float32)
        * inv_sqrt
    )
    mem_probs = masked_softmax(mem_scores, mem_mask)
    mem_out = jnp.einsum("hqk,hkd->qhd", mem_probs, mem_vals, preferred_element_type=jnp.float32)
    near_scores = (
        jnp.einsum("qhd,khd->hqk", query_heads, near_keys, preferred_element_type=jnp.float32)
        * inv_sqrt
    )
    near_probs = masked_softmax(near_scores, near_mask)
    near_out = jnp.einsum("hqk,khd->qhd", near_probs, near_vals, preferred_element_type=jnp.float32)
    gate_col = gate_value[None, :, None]
    mixed = gate_col * mem_out + (1.0 - gate_col) * near_out
    mem_grad_out = gate_col * cotangent
    near_grad_out = (1.0 - gate_col) * cotangent
    gate_terms = (
        jnp.sum(cotangent * (mem_out - near_out), axis=(0, 2)) * gate_value * (1.0 - gate_value)
    )
    mem_delta = jnp.transpose(jnp.sum(mem_grad_out * mem_out, axis=2))[:, :, None]
    near_delta = jnp.transpose(jnp.sum(near_grad_out * near_out, axis=2))[:, :, None]
    mem_grad_low = mem_grad_out.astype(jnp.bfloat16)
    near_grad_low = near_grad_out.astype(jnp.bfloat16)
    mem_dprobs = jnp.einsum(
        "qhd,hkd->hqk", mem_grad_low, mem_vals, preferred_element_type=jnp.float32
    )
    mem_dscores = (mem_probs.astype(jnp.float32) * (mem_dprobs - mem_delta) * inv_sqrt).astype(
        jnp.bfloat16
    )
    near_dprobs = jnp.einsum(
        "qhd,khd->hqk", near_grad_low, near_vals, preferred_element_type=jnp.float32
    )
    near_dscores = (near_probs.astype(jnp.float32) * (near_dprobs - near_delta) * inv_sqrt).astype(
        jnp.bfloat16
    )
    query_grad = jnp.einsum(
        "hqk,hkd->qhd", mem_dscores, mem_keys, preferred_element_type=jnp.float32
    )
    query_grad = query_grad + jnp.einsum(
        "hqk,khd->qhd", near_dscores, near_keys, preferred_element_type=jnp.float32
    )
    return (mixed, query_grad, near_dscores, near_probs, near_grad_low, gate_terms)


def regroup(pieces):
    piece_count = pieces.shape[0]
    for bit_number in range(piece_count.bit_length() - 1):
        moving_rows = jnp.asarray(
            [k for k in range(piece_count) if k >> bit_number & 1], dtype=jnp.int32
        )
        arrived = from_partner(pieces[moving_rows], "mem", bit_number)
        pieces = pieces.at[moving_rows].set(arrived)
    return pieces


def per_device(queries, local_kv, memory_kv, block_home, retrieved, stretch_pos, gate_bias, d_out):
    my_index = lax.axis_index("mem")
    per_stretch = STRETCH // TOK_DEV
    rank_in_span = my_index % per_stretch
    stretch_index = my_index // per_stretch
    block_ids_all = lax.dynamic_index_in_dim(retrieved[0], stretch_index, 0, keepdims=False)
    stretch_limit = lax.dynamic_index_in_dim(stretch_pos[0], stretch_index, 0, keepdims=False)
    gate_value = jax.nn.sigmoid(gate_bias)
    head_group = H // per_stretch
    rank_order = rank_in_span ^ jnp.arange(per_stretch, dtype=jnp.int32)
    packed = jnp.concatenate(
        [
            queries[0].reshape(TOK_DEV, 1, H, HD),
            local_kv[0].reshape(TOK_DEV, 2, H, HD),
            d_out[0].reshape(TOK_DEV, 1, H, HD),
        ],
        axis=1,
    )
    by_rank = jnp.transpose(
        packed.reshape(TOK_DEV, 4, per_stretch, head_group, HD), (2, 0, 1, 3, 4)
    )
    gathered = regroup(by_rank[rank_order])[rank_order].reshape(STRETCH, 4, head_group, HD)
    query_heads = gathered[:, 0]
    first_head = rank_in_span * head_group
    head_ids = (first_head + jnp.arange(head_group, dtype=jnp.int32))[:, None]
    block_ids = lax.dynamic_slice_in_dim(block_ids_all, first_head, head_group, 0)
    visible = (block_ids >= 0) & (block_ids < stretch_limit)
    slot_ids = block_home[0][jnp.clip(block_ids, 0, block_home.shape[1] - 1)]
    fetched = fetch_blocks(memory_kv, slot_ids, head_ids)
    positions = jnp.arange(STRETCH, dtype=jnp.int32)
    near_mask = (positions[None, :] <= positions[:, None])[None]
    gate_mine = lax.dynamic_slice_in_dim(gate_value, first_head, head_group, 0)
    cotangent = gathered[:, 3].astype(jnp.float32)
    mixed, query_grad, near_dscores, near_probs, near_grad_low, gate_terms = attend(
        query_heads,
        cotangent,
        fetched,
        visible,
        gathered[:, 1],
        gathered[:, 2],
        near_mask,
        gate_mine,
    )
    ds_blocks = near_dscores.reshape(head_group, per_stretch, TOK_DEV, STRETCH)
    probs_blocks = near_probs.reshape(head_group, per_stretch, TOK_DEV, STRETCH)
    query_blocks = query_heads.reshape(per_stretch, TOK_DEV, head_group, HD)
    cot_blocks = near_grad_low.reshape(per_stretch, TOK_DEV, head_group, HD)
    key_terms = jnp.einsum(
        "hbqk,bqhd->bkhd", ds_blocks, query_blocks, preferred_element_type=jnp.float32
    ).astype(jnp.bfloat16)
    value_terms = jnp.einsum(
        "hbqk,bqhd->bkhd", probs_blocks, cot_blocks, preferred_element_type=jnp.float32
    ).astype(jnp.bfloat16)
    key_grad = jnp.sum(key_terms.astype(jnp.float32), axis=0).astype(jnp.bfloat16)
    value_grad = jnp.sum(value_terms.astype(jnp.float32), axis=0).astype(jnp.bfloat16)
    outgoing = jnp.stack(
        [mixed.astype(jnp.bfloat16), query_grad.astype(jnp.bfloat16), key_grad, value_grad], axis=1
    )
    outgoing = outgoing.reshape(per_stretch, TOK_DEV, 4, head_group, HD)
    returned = regroup(outgoing[rank_order])[rank_order]
    results = jnp.transpose(returned, (1, 2, 0, 3, 4)).reshape(TOK_DEV, 4, H * HD)
    attended = results[:, 0][None]
    grad_queries = results[:, 1][None]
    grad_kv = results[:, 2:4][None]
    gate_full = lax.dynamic_update_slice_in_dim(
        jnp.zeros((H,), jnp.float32), gate_terms, first_head, 0
    )
    grad_gate = lax.psum(gate_full, ("mem", "dp"))
    return (attended, grad_queries, grad_kv, grad_gate)


MESH_ID = pl.DeviceIdType.MESH
SCALE = HD ** (-0.5)
CAP = 8
HG = H // 2


def dot_nt(a, b):
    return lax.dot_general(a, b, (((1,), (1,)), ((), ())), preferred_element_type=jnp.float32)


def dot_tn(a, b):
    return lax.dot_general(a, b, (((0,), (0,)), ((), ())), preferred_element_type=jnp.float32)


def dot_nn(a, b):
    return jnp.dot(a, b, preferred_element_type=jnp.float32)


def probs_of(scores):
    top = jnp.max(scores, axis=1, keepdims=True)
    lifted = jnp.exp2((scores - top) * (SCALE * 1.4426950408889634))
    return lifted * (1.0 / jnp.sum(lifted, axis=1, keepdims=True))


def layer_kernel(
    n_dp,
    q_ref,
    d_ref,
    kv_ref,
    mem_ref,
    home_ref,
    lists_ref,
    ids_ref,
    limit_ref,
    bias_ref,
    att_ref,
    dq_ref,
    gint_ref,
    gate_ref,
    gkv_v,
    qb,
    db,
    kvb,
    mem_v,
    packs,
    mask_s,
    att_s,
    dq_s,
    gkv_s,
    gx_s,
    gx,
    gate_s,
    gate_m,
    gate_d,
    send_sem,
    recv_sem,
    local_sem,
):
    me = lax.axis_index("mem")
    dp = lax.axis_index("dp")
    x = me // 2
    c = me % 2
    o = 1 - c
    mate = 2 * x + o
    far = 2 * (1 - x)
    bf = jnp.bfloat16

    def remote(src, dst, send_k, recv_k, device):
        return pltpu.make_async_remote_copy(
            src_ref=src,
            dst_ref=dst,
            send_sem=send_sem.at[send_k],
            recv_sem=recv_sem.at[recv_k],
            device_id=device,
            device_id_type=MESH_ID,
        )

    def lanes(first, count):
        return pl.ds(pl.multiple_of(first * HD, HD), count * HD)

    barrier = pltpu.get_barrier_semaphore()
    for k in range(1, 4):
        pl.semaphore_signal(
            barrier, inc=1, device_id={"mem": (me + k) % 4}, device_id_type=MESH_ID
        )
    for k in range(1, n_dp):
        pl.semaphore_signal(
            barrier, inc=1, device_id={"dp": (dp + k) % n_dp}, device_id_type=MESH_ID
        )

    locals_ = [
        pltpu.make_async_copy(q_ref.at[:, lanes(c * HG, HG)], qb.at[c], local_sem.at[0]),
        pltpu.make_async_copy(d_ref.at[:, lanes(c * HG, HG)], db.at[c], local_sem.at[1]),
        pltpu.make_async_copy(kv_ref.at[pl.ds(c * HG, HG)], kvb.at[me], local_sem.at[2]),
        pltpu.make_async_copy(mem_ref, mem_v, local_sem.at[3]),
    ]
    for copy in locals_:
        copy.start()

    slots = 2 * 4

    def stored_flags(index):
        flags = []
        for low in range(2):
            block = jnp.int32(0)
            for r in range(slots):
                block = jnp.where(home_ref[0, r] == 2 * index + low, r, block)
            seen = block < limit_ref[0, 0]
            for h in range(H):
                found = ids_ref[0, 0, h, 0] == block
                for j in range(1, slots):
                    found = found | (ids_ref[0, 0, h, j] == block)
                flags.append(jnp.where(found & seen, 1, 0))
        return flags

    def places(flags):
        count = jnp.int32(0)
        result = []
        for flag in flags:
            result.append(count)
            count = count + flag
        return result

    mine = stored_flags(me)
    mine_at = places(mine)
    chosen = []
    for k in range(CAP):
        entry = jnp.int32(0)
        for e in range(2 * H):
            entry = jnp.where((mine[e] == 1) & (mine_at[e] == k), e, entry)
        chosen.append(entry)
    locals_[3].wait()
    for k in range(CAP):
        packs[me, k] = mem_v[chosen[k]]

    pl.semaphore_wait(barrier, 2 + n_dp)

    core_copies = [
        remote(q_ref.at[:, lanes(o * HG, HG)], qb.at[c], 0, 0, {"mem": mate}),
        remote(d_ref.at[:, lanes(o * HG, HG)], db.at[c], 1, 1, {"mem": mate}),
        remote(kv_ref.at[pl.ds(o * HG, HG)], kvb.at[me], 2, 2, {"mem": mate}),
        remote(packs.at[me], packs.at[me], 3, 3, {"mem": mate}),
    ]

    def kv_copy(to, hh):
        return remote(
            kv_ref.at[to * HG + hh],
            kvb.at[me, hh],
            4 + to * HG + hh,
            4 + c * HG + hh,
            {"mem": far + to},
        )

    for copy in core_copies[:3]:
        copy.start()
    pack_copy = remote(packs.at[me], packs.at[me], 12, 12, {"mem": far + c})
    pack_copy.start()

    @pl.when(x == 0)
    def _():
        for hh in range(HG):
            for to in range(2):
                kv_copy(to, hh).start()

    core_copies[3].start()

    key_slot = lax.broadcasted_iota(jnp.int32, (H, slots * 64), 1) // 64
    block_of = jnp.zeros((H, slots * 64), jnp.int32)
    for r in range(slots):
        block_of = jnp.where(key_slot == home_ref[0, r], r, block_of)
    named = jnp.zeros((H, slots * 64), jnp.bool_)
    for j in range(slots):
        named = named | (block_of == lists_ref[0, 0, :, j : j + 1])
    mask_s[...] = jnp.where(named & (block_of < limit_ref[0, 0]), 0.0, neg_large)
    gate_s[...] = jnp.zeros_like(gate_s)

    def res_copy(kind, hh):
        head = c * HG + hh
        if kind == 0:
            return remote(
                att_s.at[o, hh], att_ref.at[:, lanes(head, 1)], 20 + hh, 20 + hh, {"mem": mate}
            )
        if kind == 1:
            return remote(
                dq_s.at[o, hh], dq_ref.at[:, lanes(head, 1)], 24 + hh, 24 + hh, {"mem": mate}
            )
        return remote(gkv_s.at[o, hh], gkv_v.at[head], 28 + hh, 28 + hh, {"mem": mate})

    def gx_copy(to, hh):
        return remote(
            gx_s.at[to, hh],
            gx.at[c * HG + hh],
            32 + to * HG + hh,
            32 + c * HG + hh,
            {"mem": far + to},
        )

    def own_copy(kind, hh):
        head = c * HG + hh
        sem = local_sem.at[4 + kind * HG + hh]
        if kind == 0:
            return pltpu.make_async_copy(att_s.at[c, hh], att_ref.at[:, lanes(head, 1)], sem)
        if kind == 1:
            return pltpu.make_async_copy(dq_s.at[c, hh], dq_ref.at[:, lanes(head, 1)], sem)
        return pltpu.make_async_copy(gkv_s.at[c, hh], gkv_v.at[head], sem)

    at = []
    for index in range(4):
        at.append([jnp.minimum(place, CAP - 1) for place in places(stored_flags(index))])

    def entry_place(index, low, hh):
        return jnp.where(c == 0, at[index][low * H + hh], at[index][low * H + HG + hh])

    for copy in locals_[:3]:
        copy.wait()
    for copy in core_copies:
        copy.wait_recv()
    pack_copy_in = remote(packs.at[me], packs.at[far + c], 12, 12, {"mem": mate})
    pack_copy_in.wait_recv()
    forward = remote(packs.at[far + c], packs.at[far + c], 13, 13, {"mem": mate})
    forward.start()
    remote(packs.at[me], packs.at[far + o], 13, 13, {"mem": mate}).wait_recv()

    gate_mem = [
        remote(gate_s, gate_m.at[k - 1], 40 + k, 40 + k, {"mem": (me + k) % 4})
        for k in range(1, 4)
    ]
    gate_dp = [
        remote(gate_d.at[0], gate_d.at[k], 43 + k, 43 + k, {"dp": (dp + k) % n_dp})
        for k in range(1, n_dp)
    ]

    def gate_step():
        for copy in gate_mem:
            copy.wait()
        gate_d[0] = gate_s[...] + gate_m[0] + gate_m[1] + gate_m[2]
        for copy in gate_dp:
            copy.start()

    def one_head(hh, later):
        rows = 2 * TOK_DEV
        keys_n = 2 * TOK_DEV * (1 + later)
        head = c * HG + hh
        query = qb[:, :, hh * HD : (hh + 1) * HD].reshape(rows, HD)
        dout = db[:, :, hh * HD : (hh + 1) * HD].reshape(rows, HD).astype(jnp.float32)
        gate = 1.0 / (1.0 + jnp.exp(-jnp.full((1, HD), bias_ref[head], jnp.float32)))
        mem_cot = gate * dout
        near_cot = (1.0 - gate) * dout
        near_cot16 = near_cot.astype(bf)

        entries = [
            packs[index, entry_place(index, low, hh)] for index in range(4) for low in range(2)
        ]
        mem_keys = jnp.concatenate([entry[0] for entry in entries], axis=0)
        mem_vals = jnp.concatenate([entry[1] for entry in entries], axis=0)
        mem_probs = probs_of(dot_nt(query, mem_keys) + mask_s[pl.ds(head, 1), :])
        mem_out = dot_nn(mem_probs.astype(bf), mem_vals)
        mem_delta = jnp.sum(mem_cot * mem_out, axis=1, keepdims=True)
        mem_ds = (
            mem_probs * (dot_nt((mem_cot * SCALE).astype(bf), mem_vals) - mem_delta * SCALE)
        ).astype(bf)
        query_grad = dot_nn(mem_ds, mem_keys)

        if later:
            for frm in range(2):
                remote(
                    kv_ref.at[0], kvb.at[frm, hh], 0, 4 + frm * HG + hh, {"mem": mate}
                ).wait_recv()
            near_keys = kvb[:, hh, 0].reshape(keys_n, HD)
            near_vals = kvb[:, hh, 1].reshape(keys_n, HD)
        else:
            near_keys = kvb[0:2, hh, 0].reshape(keys_n, HD)
            near_vals = kvb[0:2, hh, 1].reshape(keys_n, HD)
        row = lax.broadcasted_iota(jnp.int32, (rows, keys_n), 0)
        col = lax.broadcasted_iota(jnp.int32, (rows, keys_n), 1)
        causal = col <= row + (keys_n - rows)
        near_probs = probs_of(
            jnp.where(causal, dot_nt(query, near_keys), neg_large)
        )
        near_low = near_probs.astype(bf)
        near_out = dot_nn(near_low, near_vals)
        gate_s[pl.ds(head, 1), :] = (
            jnp.sum(dout * (mem_out - near_out), axis=0, keepdims=True) * gate * (1.0 - gate)
        )
        if hh == HG - 1:
            for copy in gate_mem:
                copy.start()
        near_delta = jnp.sum(near_cot * near_out, axis=1, keepdims=True)
        near_ds = (
            near_probs * (dot_nt((near_cot * SCALE).astype(bf), near_vals) - near_delta * SCALE)
        ).astype(bf)
        key_grad = dot_tn(near_ds, query).astype(bf)
        val_grad = dot_tn(near_low, near_cot16).astype(bf)
        split = keys_n - rows
        if later:
            gx_s[:, hh, 0] = key_grad[:split].reshape(2, TOK_DEV, HD)
            gx_s[:, hh, 1] = val_grad[:split].reshape(2, TOK_DEV, HD)
            for to in range(2):
                gx_copy(to, hh).start()
        gkv_s[:, hh, 0] = key_grad[split:].reshape(2, TOK_DEV, HD)
        gkv_s[:, hh, 1] = val_grad[split:].reshape(2, TOK_DEV, HD)
        mixed = (gate * mem_out + (1.0 - gate) * near_out).astype(bf)
        att_s[:, hh] = mixed.reshape(2, TOK_DEV, HD)
        if later and hh == HG - 1:
            gate_step()
        query_grad = query_grad + dot_nn(near_ds, near_keys)
        dq_s[:, hh] = query_grad.astype(bf).reshape(2, TOK_DEV, HD)
        for kind in range(3):
            res_copy(kind, hh).start()
            own_copy(kind, hh).start()

    @pl.when(x == 0)
    def _():
        for hh in range(HG):
            one_head(hh, False)
        gate_step()

    @pl.when(x == 1)
    def _():
        for hh in range(HG):
            one_head(hh, True)

    for kind in range(3):
        for hh in range(HG):
            own_copy(kind, hh).wait()
            copy = res_copy(kind, hh)
            copy.wait_send()
    for hh in range(HG):
        other = o * HG + hh
        remote(
            att_s.at[0, 0], att_ref.at[:, lanes(other, 1)], 0, 20 + hh, {"mem": mate}
        ).wait_recv()
        remote(
            dq_s.at[0, 0], dq_ref.at[:, lanes(other, 1)], 0, 24 + hh, {"mem": mate}
        ).wait_recv()
        remote(gkv_s.at[0, 0], gkv_v.at[other], 0, 28 + hh, {"mem": mate}).wait_recv()

    def join_pairs(head, both):
        gint_ref[:, :, head * HD : (head + 1) * HD] = jnp.stack([both[0], both[1]], axis=1)

    @pl.when(x == 0)
    def _():
        for hh in range(HG):
            for to in range(2):
                kv_copy(to, hh).wait_send()
        for hh in range(HG):
            for frm in range(2):
                head = frm * HG + hh
                remote(
                    gkv_s.at[0, 0], gx.at[head], 0, 32 + head, {"mem": mate}
                ).wait_recv()
                both = gkv_v[head].astype(jnp.float32) + gx[head].astype(jnp.float32)
                join_pairs(head, both.astype(bf))

    @pl.when(x == 1)
    def _():
        for head in range(H):
            join_pairs(head, gkv_v[head])
        for hh in range(HG):
            for to in range(2):
                gx_copy(to, hh).wait_send()

    pack_copy.wait_send()
    forward.wait_send()
    for copy in core_copies:
        copy.wait_send()
    for copy in gate_dp:
        copy.wait()
    total = gate_d[0]
    for k in range(1, n_dp):
        total = total + gate_d[k]
    summed = jnp.broadcast_to(jnp.sum(total, axis=1, keepdims=True), (H, HD))
    eye = lax.broadcasted_iota(jnp.int32, (H, HD), 0) == lax.broadcasted_iota(
        jnp.int32, (H, HD), 1
    )
    gate_ref[...] = jnp.sum(jnp.where(eye, summed, 0.0), axis=0, keepdims=True)


def one_stretch_per_document(
    n_dp, queries, local_kv, memory_kv, block_home, retrieved, stretch_pos, gate_bias, d_out
):
    bf = jnp.bfloat16
    kv_heads = jnp.transpose(local_kv.reshape(TOK_DEV, 2, H, HD), (2, 1, 0, 3))
    vmem = pl.BlockSpec(memory_space=pltpu.VMEM)
    smem = pl.BlockSpec(memory_space=pltpu.SMEM)
    hbm = pl.BlockSpec(memory_space=pl.ANY)
    n_sems = 44 + n_dp
    attended, grad_queries, grad_kv, grad_gate = pl.pallas_call(
        functools.partial(layer_kernel, n_dp),
        out_shape=(
            jax.ShapeDtypeStruct((TOK_DEV, H * HD), bf),
            jax.ShapeDtypeStruct((TOK_DEV, H * HD), bf),
            jax.ShapeDtypeStruct((TOK_DEV, 2, H * HD), bf),
            jax.ShapeDtypeStruct((1, HD), jnp.float32),
        ),
        in_specs=[hbm, hbm, vmem, hbm, smem, vmem, smem, smem, smem],
        out_specs=(vmem, vmem, vmem, vmem),
        scratch_shapes=[
            pltpu.VMEM((H, 2, TOK_DEV, HD), bf),
            pltpu.VMEM((2, TOK_DEV, HG * HD), bf),
            pltpu.VMEM((2, TOK_DEV, HG * HD), bf),
            pltpu.VMEM((4, HG, 2, TOK_DEV, HD), bf),
            pltpu.VMEM((2 * H, 2, 64, HD), bf),
            pltpu.VMEM((4, CAP, 2, 64, HD), bf),
            pltpu.VMEM((H, 512), jnp.float32),
            pltpu.VMEM((2, HG, TOK_DEV, HD), bf),
            pltpu.VMEM((2, HG, TOK_DEV, HD), bf),
            pltpu.VMEM((2, HG, 2, TOK_DEV, HD), bf),
            pltpu.VMEM((2, HG, 2, TOK_DEV, HD), bf),
            pltpu.VMEM((H, 2, TOK_DEV, HD), bf),
            pltpu.VMEM((H, HD), jnp.float32),
            pltpu.VMEM((3, H, HD), jnp.float32),
            pltpu.VMEM((n_dp, H, HD), jnp.float32),
            pltpu.SemaphoreType.DMA((n_sems,)),
            pltpu.SemaphoreType.DMA((n_sems,)),
            pltpu.SemaphoreType.DMA((4 + 3 * HG,)),
        ],
        compiler_params=pltpu.CompilerParams(
            collective_id=0, has_side_effects=True, vmem_limit_bytes=40 * 1024 * 1024
        ),
    )(
        queries[0],
        d_out[0],
        kv_heads,
        memory_kv[0].reshape(2 * H, 2, 64, HD),
        block_home,
        retrieved,
        retrieved,
        stretch_pos,
        gate_bias,
    )
    return (attended[None], grad_queries[None], grad_kv[None], grad_gate[0, :H])


def solution(mesh):
    body = per_device
    if mesh.shape["mem"] == STRETCH // TOK_DEV:
        body = functools.partial(one_stretch_per_document, mesh.shape["dp"])
    in_specs = (
        P(("groups", "dp"), "mem", None),
        P(("groups", "dp"), "mem", None, None),
        P(("groups", "dp"), "mem", None, None, None, None),
        P(("groups", "dp"), None),
        P(("groups", "dp"), None, None, None),
        P(("groups", "dp"), None),
        P(),
        P(("groups", "dp"), "mem", None),
    )
    out_specs = (
        P(("groups", "dp"), "mem", None),
        P(("groups", "dp"), "mem", None),
        P(("groups", "dp"), "mem", None, None),
        P("groups"),
    )
    return jax.shard_map(
        body, mesh=mesh, in_specs=in_specs, out_specs=out_specs, check_vma=False
    )
```
